32 devices in a mesh: dp: 8 (over y, x, core), seq: 4 (over z).
Axes of the slice: x: 2, y: 2, z: 4, core: 2. Of those that a mesh axis runs over, the one named last changes fastest.
Arguments:
- queries: bfloat16 [8, 512, 4096], P('dp', 'seq'), may hold values from -30 to 30
- keys: bfloat16 [8, 512, 1024], P('dp', 'seq'), may hold values from -6 to 6
- values: bfloat16 [8, 512, 1024], P('dp', 'seq'), may hold values from -6 to 6
- head_weight: bfloat16 [4096, 256], P('dp'), may hold values from -0.5 to 0.5
- value_weight: bfloat16 [4096], P('dp'), may hold values from -0.5 to 0.5
- action_ids: int32 [8, 512], P('dp', 'seq'), may hold values from 0 to 255
- rewards: int32 [8, 512], P('dp', 'seq'), may hold values from -128 to 127
- episode_ids: int32 [8, 4], P('dp'), may hold values from 0 to 2, never falling along the last dimension, each value on 1 to 2 neighbouring positions
Outputs:
- grad_queries: bfloat16 [8, 512, 4096], P('dp', 'seq')
- grad_keys: bfloat16 [8, 512, 1024], P('dp', 'seq')
- grad_values: bfloat16 [8, 512, 1024], P('dp', 'seq')
- grad_head: float32 [4096, 256], P('dp')
- grad_value: float32 [4096], P('dp')
The draws below stay inside these ranges and needn't reach their ends.
Inputs may be any that keep to these rules, and one draw needn't show every extreme that they name: `episode_ids`: episode numbers never fall along a row; each episode covers 1 to 2 whole blocks, one exactly 2.
All inputs are finite; a program needn't handle non-finite values.
Results may differ from the reference program's by a relative error of at most 0.01.
Values may be sent and summed in bfloat16 or wider, within the bound.
A program may use at most 128 MiB of HBM per device.

```python
import math
import jax
import jax.numpy as jnp
import numpy as np
from jax import lax

HEADS = 32
KV_HEADS = 8
HD = 128
ACTS = 256
BLOCK = 128
ROWS = 8
LENGTH = 512
NBLK = 4
QW = 4096
KVW = 1024
EP_MOST = 2
EPISODES = 3


def shared_keys(key):
    return jnp.clip(jax.random.normal(key, (ROWS, LENGTH, KV_HEADS * HD), jnp.float32), -6.0, 6.0)


def draw_keys(key, part):
    return shared_keys(key).astype(jnp.bfloat16)


def draw_queries(key, part):
    key = jax.random.fold_in(key, 7)
    noise_key = jax.random.fold_in(key, 0)
    queries = jnp.clip(jax.random.normal(noise_key, (ROWS, LENGTH, HEADS * HD), jnp.float32), -6.0, 6.0)
    return queries.astype(jnp.bfloat16)


def plant(drawn, own_key, smallest, high):
    spot = [jax.random.randint(jax.random.fold_in(own_key, axis), (), 0, length) for axis, length in enumerate(drawn.shape)]
    main_axis = drawn.shape.index(max(drawn.shape))
    next_to = spot[:main_axis] + [(spot[main_axis] + 1) % drawn.shape[main_axis]] + spot[main_axis + 1:]
    return drawn.at[tuple(spot)].set(smallest).at[tuple(next_to)].set(high)


def steps_of(stream_key, extent, pieces, least, largest):
    loudness = 1.0
    for position, shards_of in pieces:
        steps = jax.random.uniform(jax.random.fold_in(jax.random.fold_in(stream_key, 6), position), (shards_of,), jnp.float32, least / len(pieces), largest / len(pieces))
        loudness = loudness * jnp.repeat(jnp.exp(steps), extent[position] // shards_of).reshape((-1,) + (1,) * (len(extent) - 1 - position))
    return loudness


def rank_table(amount, skew):
    weights = [(1 << 20) // math.isqrt(standing ** skew) + 1 for standing in range(1, amount + 1)]
    deviation = 1 + sum(weights) // (1 << 30)
    return np.cumsum(np.array([max(1, weight // deviation) for weight in weights]))


def ranked_ids(key, extent, number_of, slope):
    table = rank_table(number_of, slope)
    lot = jax.random.randint(jax.random.fold_in(key, 1), extent, 0, int(table[number_of - 1]))
    grade = jnp.searchsorted(jnp.asarray(table, jnp.int32), lot, side="right")
    return jax.random.permutation(jax.random.fold_in(key, 2), number_of)[grade].astype(jnp.int32)


def split_up(count, total, limit, lean):
    portions = [(1 << 20) // math.isqrt(standing ** lean) + 1 for standing in range(2, count + 1)]
    spare, holding = total - limit - (count - 1), [1] * (count - 1)
    while spare > 0:
        candidates = [i for i in range(count - 1) if holding[i] < limit]
        pool, left = sum([portions[i] for i in candidates]), spare
        for i in candidates:
            more = min(limit - holding[i], max(1, left * portions[i] // pool), spare)
            holding[i] = holding[i] + more
            spare = spare - more
    return np.array([limit] + holding)


def uneven_parts(own_key, number_of, total, bound, slope):
    if number_of == 2:
        one = jax.random.randint(own_key, (), max(1, total - bound), min(bound, total - 1) + 1)
        return jnp.stack([one, total - one])
    sizes = jnp.asarray(split_up(number_of, total, bound, slope), jnp.int32)
    pairs = (number_of - 1) // 2
    giver, sink = sizes[1:1 + 2 * pairs:2], sizes[2:2 + 2 * pairs:2]
    slack = jnp.minimum(giver - 1, bound - sink)
    moved = jax.random.randint(jax.random.fold_in(own_key, 1), (pairs,), 0, 1 << 20) % (slack + 1)
    sizes = sizes.at[1:1 + 2 * pairs:2].set(giver - moved).at[2:2 + 2 * pairs:2].set(sink + moved)
    return sizes[jax.random.permutation(jax.random.fold_in(own_key, 2), number_of)]


def scatter_about(own_key, dims, scale, bound, cuts=(), dtype=jnp.bfloat16):
    entries = jax.random.normal(own_key, dims, jnp.float32) * scale
    if len(cuts) > 0:
        entries = steps_of(own_key, dims, cuts, -0.22, 0.18) * entries
    return jnp.clip(entries, min=-bound, max=bound).astype(dtype)


def setup_inputs(seed: int = 0) -> dict:
    streams_of = jax.random.split(jax.random.key(seed), 9)
    queries = draw_queries(jax.random.fold_in(streams_of[8], 71), 0)
    keys = draw_keys(jax.random.fold_in(streams_of[8], 71), 0)
    values = scatter_about(streams_of[2], (ROWS, LENGTH, KVW), 1.0, 6.0, ((0, 8), (1, 4)))
    head_weight = scatter_about(streams_of[3], (QW, ACTS), HD ** -0.5, 0.5, ((0, 8),))
    value_weight = scatter_about(streams_of[4], (QW,), HD ** -0.5, 0.5, ((0, 8),))
    action_ids = plant(ranked_ids(streams_of[5], (ROWS, LENGTH), ACTS, 2), jax.random.fold_in(streams_of[5], 3), 0, ACTS - 1).astype(jnp.int32)
    rewards = plant(jax.random.randint(streams_of[6], (ROWS, LENGTH), -128, 128), jax.random.fold_in(streams_of[6], 1), -128, 127).astype(jnp.int32)
    episode_ids = jax.vmap(lambda own: jnp.searchsorted(jnp.cumsum(uneven_parts(own, EPISODES, NBLK, EP_MOST, 2)), jnp.arange(NBLK), side="right"))(jax.random.split(streams_of[7], ROWS)).reshape((ROWS, NBLK)).astype(jnp.int32)
    return dict(queries=queries, keys=keys, values=values, head_weight=head_weight, value_weight=value_weight, action_ids=action_ids, rewards=rewards, episode_ids=episode_ids)


GAMMA = 0.99
TAU = 0.7
REWARD_UNIT = 64.0
NEG_FILL = -1e30


def group_probs(q_group, k_head, allowed, scale):
    scores = jnp.einsum("gtd,sd->gts", q_group.astype(jnp.float32), k_head.astype(jnp.float32), precision=lax.Precision.HIGHEST) * scale
    scores = jnp.where(allowed[None], scores, NEG_FILL)
    top = jnp.max(scores, axis=-1, keepdims=True)
    expo = jnp.exp(scores - top)
    probs = expo / jnp.sum(expo, axis=-1, keepdims=True)
    return probs, probs.astype(jnp.bfloat16)


def reference(queries, keys, values, head_weight, value_weight, action_ids, rewards, episode_ids):
    rows, length, qwidth = queries.shape
    group = HEADS // KV_HEADS
    scale = HD ** -0.5
    positions = jnp.arange(length)

    def one_row(carry, inputs):
        q_row, k_row, v_row, act_row, rew_row, ep_row = inputs
        tok_episode = jnp.repeat(ep_row, BLOCK)
        allowed = (positions[None, :] <= positions[:, None]) & (tok_episode[None, :] == tok_episode[:, None])
        q_group = q_row.reshape(length, KV_HEADS, group, HD).transpose(1, 2, 0, 3)
        k_group = k_row.reshape(length, KV_HEADS, HD).transpose(1, 0, 2)
        v_group = v_row.reshape(length, KV_HEADS, HD).transpose(1, 0, 2)

        def forward(args):
            q_one, k_one, v_one = args
            probs, probs_low = group_probs(q_one, k_one, allowed, scale)
            mixed = jnp.einsum("gts,sd->tgd", probs_low.astype(jnp.float32), v_one.astype(jnp.float32), precision=lax.Precision.HIGHEST)
            return mixed.astype(jnp.bfloat16)

        mixed = lax.map(forward, (q_group, k_group, v_group))
        attended = mixed.transpose(1, 0, 2, 3).reshape(length, qwidth)
        q_all = jnp.dot(attended, head_weight, preferred_element_type=jnp.float32)
        onehot = (act_row[:, None] == jnp.arange(ACTS)[None, :]).astype(jnp.float32)
        q_taken = jnp.sum(q_all * onehot, axis=1)
        v_now = jnp.dot(attended, value_weight, preferred_element_type=jnp.float32)
        same = (tok_episode[1:] == tok_episode[:-1]).astype(jnp.float32)
        v_next = jnp.concatenate([v_now[1:] * same, jnp.zeros((1,), jnp.float32)])
        target = rew_row.astype(jnp.float32) / REWARD_UNIT + GAMMA * v_next
        err = q_taken - target
        gap = q_taken - v_now
        weight = jnp.where(gap < 0, 1.0 - TAU, TAU)
        grad_q = (2.0 * err).astype(jnp.bfloat16)
        grad_v = (-2.0 * weight * gap).astype(jnp.bfloat16)
        select = (onehot * grad_q.astype(jnp.float32)[:, None]).astype(jnp.bfloat16)
        grad_att = jnp.dot(select, head_weight.T, preferred_element_type=jnp.float32)
        grad_att = (grad_att + grad_v.astype(jnp.float32)[:, None] * value_weight.astype(jnp.float32)[None, :]).astype(jnp.bfloat16)
        head_part = jnp.dot(attended.T, select, preferred_element_type=jnp.float32)
        value_part = jnp.dot(grad_v, attended, preferred_element_type=jnp.float32)
        d_group = grad_att.reshape(length, KV_HEADS, group, HD).transpose(1, 2, 0, 3)

        def backward(args):
            q_one, k_one, v_one, d_one = args
            probs, probs_low = group_probs(q_one, k_one, allowed, scale)
            d_probs = jnp.einsum("gtd,sd->gts", d_one.astype(jnp.float32), v_one.astype(jnp.float32), precision=lax.Precision.HIGHEST)
            delta = jnp.sum(probs * d_probs, axis=-1, keepdims=True)
            d_scores = (probs * (d_probs - delta) * scale).astype(jnp.bfloat16)
            grad_q_one = jnp.einsum("gts,sd->tgd", d_scores.astype(jnp.float32), k_one.astype(jnp.float32), precision=lax.Precision.HIGHEST)
            grad_k_one = jnp.einsum("gts,gtd->sd", d_scores.astype(jnp.float32), q_one.astype(jnp.float32), precision=lax.Precision.HIGHEST)
            grad_v_one = jnp.einsum("gts,gtd->sd", probs_low.astype(jnp.float32), d_one.astype(jnp.float32), precision=lax.Precision.HIGHEST)
            return grad_q_one.astype(jnp.bfloat16), grad_k_one.astype(jnp.bfloat16), grad_v_one.astype(jnp.bfloat16)

        dq_group, dk_group, dv_group = lax.map(backward, (q_group, k_group, v_group, d_group))
        dq_row = dq_group.transpose(1, 0, 2, 3).reshape(length, qwidth)
        dk_row = dk_group.transpose(1, 0, 2).reshape(length, KV_HEADS * HD)
        dv_row = dv_group.transpose(1, 0, 2).reshape(length, KV_HEADS * HD)
        return (carry[0] + head_part, carry[1] + value_part), (dq_row, dk_row, dv_row)

    init = (jnp.zeros((qwidth, ACTS), jnp.float32), jnp.zeros((qwidth,), jnp.float32))
    sums, grads = lax.scan(one_row, init, (queries, keys, values, action_ids, rewards, episode_ids))
    return grads[0], grads[1], grads[2], sums[0], sums[1]
```

```python
import jax
import jax.numpy as jnp
from jax import lax
from jax.sharding import PartitionSpec as P

HEADS = 32
KV_HEADS = 8
HD = 128
ACTS = 256
BLOCK = 128


GAMMA = 0.99
TAU = 0.7
REWARD_UNIT = 64.0
NEG_FILL = -1e30


def passed_along(x, axis, by):
    count = lax.axis_size(axis)
    pairs = [(i, i + by) for i in range(count) if 0 <= i + by < count]
    return lax.ppermute(x, axis, pairs)


def loss_grads(q_taken, v_now, v_next, reward_row):
    target = reward_row.astype(jnp.float32) / REWARD_UNIT + GAMMA * v_next
    err = q_taken - target
    gap = q_taken - v_now
    weight = jnp.where(gap < 0, 1.0 - TAU, TAU)
    grad_q = (2.0 * err).astype(jnp.bfloat16)
    grad_v = (-2.0 * weight * gap).astype(jnp.bfloat16)
    return (grad_q, grad_v)


def per_device(queries, keys, values, head_weight, value_weight, action_ids, rewards, episode_ids):
    tok_local = queries.shape[1]
    group = HEADS // KV_HEADS
    scale = HD ** (-0.5)
    me = lax.axis_index("seq")
    both = jnp.concatenate([keys[0], values[0]], axis=1)
    before = passed_along(both, "seq", 1)
    weight_full, value_full = (
        lax.all_gather(head_weight, "dp", axis=0, tiled=True),
        lax.all_gather(value_weight, "dp", axis=0, tiled=True),
    )
    episodes = episode_ids[0]
    mine = lax.dynamic_index_in_dim(episodes, me, keepdims=False)
    padded = jnp.concatenate([jnp.full((1,), -1, jnp.int32), episodes, jnp.full((1,), -1, jnp.int32)])
    linked_before = lax.dynamic_index_in_dim(padded, me, keepdims=False) == mine
    linked_after = lax.dynamic_index_in_dim(padded, me + 2, keepdims=False) == mine
    pair = jnp.concatenate([before, both], axis=0)
    width = KV_HEADS * HD
    k_heads = pair[:, :width].reshape(2 * tok_local, KV_HEADS, HD)
    v_heads = pair[:, width:].reshape(2 * tok_local, KV_HEADS, HD)
    q_heads = queries[0].reshape(tok_local, KV_HEADS, group, HD)
    at = jnp.arange(tok_local)
    allowed = jnp.concatenate(
        [jnp.broadcast_to(linked_before, (tok_local, tok_local)), at[None, :] <= at[:, None]], axis=1
    )
    scores = (
        jnp.einsum("tmgd,smd->mgts", q_heads, k_heads, preferred_element_type=jnp.float32) * scale
    )
    scores = jnp.where(allowed, scores, NEG_FILL)
    top = jnp.max(scores, axis=-1, keepdims=True)
    expo = jnp.exp(scores - top)
    probs = expo / jnp.sum(expo, axis=-1, keepdims=True)
    probs_low = probs.astype(jnp.bfloat16)
    mixed = jnp.einsum("mgts,smd->tmgd", probs_low, v_heads, preferred_element_type=jnp.float32)
    attended = mixed.astype(jnp.bfloat16).reshape(tok_local, HEADS * HD)
    shared = lax.all_to_all(attended, "dp", split_axis=1, concat_axis=0, tiled=True)
    q_all = jnp.dot(attended, weight_full, preferred_element_type=jnp.float32)
    onehot = (action_ids[0][:, None] == jnp.arange(ACTS)[None, :]).astype(jnp.float32)
    q_taken = jnp.sum(q_all * onehot, axis=1)
    v_now = jnp.dot(attended, value_full, preferred_element_type=jnp.float32)
    v_after = passed_along(v_now[:1], "seq", -1)
    v_after = jnp.where(linked_after, v_after, 0.0)
    v_next = jnp.concatenate([v_now[1:], v_after])
    grad_q, grad_v = loss_grads(q_taken, v_now, v_next, rewards[0])
    select = (onehot * grad_q.astype(jnp.float32)[:, None]).astype(jnp.bfloat16)
    grad_att = jnp.dot(select, weight_full.T, preferred_element_type=jnp.float32)
    grad_att = (
        grad_att + grad_v.astype(jnp.float32)[:, None] * value_full.astype(jnp.float32)[None, :]
    ).astype(jnp.bfloat16)
    steer = jnp.concatenate([select, grad_v[:, None]], axis=1)
    steer_all = lax.all_gather(steer, "dp", axis=0, tiled=True)
    part = jnp.dot(shared.T, steer_all, preferred_element_type=jnp.float32)
    part = lax.psum(part, "seq")
    grad_head, grad_value = part[:, :ACTS], part[:, ACTS]
    d_heads = grad_att.reshape(tok_local, KV_HEADS, group, HD)
    d_probs = jnp.einsum("tmgd,smd->mgts", d_heads, v_heads, preferred_element_type=jnp.float32)
    delta = jnp.sum(probs * d_probs, axis=-1, keepdims=True)
    d_scores = (probs * (d_probs - delta) * scale).astype(jnp.bfloat16)
    query_grad = jnp.einsum("mgts,smd->tmgd", d_scores, k_heads, preferred_element_type=jnp.float32)
    key_sum = jnp.einsum("mgts,tmgd->smd", d_scores, q_heads, preferred_element_type=jnp.float32)
    value_sum = jnp.einsum("mgts,tmgd->smd", probs_low, d_heads, preferred_element_type=jnp.float32)
    sums = jnp.concatenate(
        [key_sum.reshape(2 * tok_local, width), value_sum.reshape(2 * tok_local, width)], axis=1
    )
    later = passed_along(sums[:tok_local].astype(jnp.bfloat16), "seq", -1)
    sums = (sums[tok_local:] + later.astype(jnp.float32)).astype(jnp.bfloat16)
    query_low = query_grad.astype(jnp.bfloat16).reshape(tok_local, HEADS * HD)
    return (query_low[None], sums[None, :, :width], sums[None, :, width:], grad_head, grad_value)


def solution(mesh):
    return jax.shard_map(
        per_device,
        mesh=mesh,
        in_specs=(
            P("dp", "seq", None),
            P("dp", "seq", None),
            P("dp", "seq", None),
            P("dp", None),
            P("dp"),
            P("dp", "seq"),
            P("dp", "seq"),
            P("dp", None),
        ),
        out_specs=(
            P("dp", "seq", None),
            P("dp", "seq", None),
            P("dp", "seq", None),
            P("dp", None),
            P("dp"),
        ),
        check_vma=False,
    )
```

```python
import functools

import jax
import jax.numpy as jnp
from jax import lax
from jax.experimental import pallas as pl
from jax.experimental.pallas import tpu as pltpu
from jax.sharding import PartitionSpec as P

HEADS = 32
KV_HEADS = 8
HD = 128
ACTS = 256
BLOCK = 128
GROUP = HEADS // KV_HEADS
GW = GROUP * HD

GAMMA = 0.99
TAU = 0.7
REWARD_UNIT = 64.0
NEG_FILL = -1e30
SCALE = HD ** (-0.5)

F32 = jnp.float32
BF16 = jnp.bfloat16
MESH = pl.DeviceIdType.MESH

NT = (((1,), (1,)), ((), ()))
NN = (((1,), (0,)), ((), ()))
TN = (((0,), (0,)), ((), ()))


def mul(a, b, dims):
    return lax.dot_general(a, b, dims, preferred_element_type=F32)


def stacked(x):
    return jnp.concatenate([x[:, i * HD : (i + 1) * HD] for i in range(GROUP)], axis=0)


def side_by_side(x):
    return jnp.concatenate([x[i * BLOCK : (i + 1) * BLOCK] for i in range(GROUP)], axis=1)


def kernel(
    D, S, FL,
    q_ref, k_ref, v_ref, hw_ref, vw_ref, act_ref, rew_ref, ep_ref,
    dq_ref, dk_ref, dv_ref, gh_ref, gv_ref,
    kprev, vprev, hw_all, vw_all, bias, probs, att, shared, q_acc, v_acc, v_out, v_in,
    sel, gvb, steer, sel_t, dks, dvs, dkr, dvr, dka, dva, part, pre_in, pre_out, suf_in, suf_out,
    k_s, k_r, v_s, v_r, hw_s, hw_f, hw_r, vw_s, vw_r, at_s, at_r, st_s, st_r, vn_s, vn_r,
    dk_s, dk_r, dv_s, dv_r, pre_s, pre_r, suf_s, suf_r,
):
    dp = lax.axis_index("dp")
    sq = lax.axis_index("seq")
    sib = dp + 1 - 2 * (dp % 2)
    R = GW // FL
    rows = ACTS + 16
    cuts = ((0, 128), (128, rows - 128))

    def copy(src, dst, ss, rs, where):
        return pltpu.make_async_remote_copy(
            src_ref=src, dst_ref=dst, send_sem=ss, recv_sem=rs, device_id=where, device_id_type=MESH
        )

    def order(j):
        if R == 1:
            return (dp + j - 2 * (dp % 2) * (j % 2) + D) % D
        return (dp // R + j) % KV_HEADS

    def lanes(i, width):
        return pl.ds(pl.multiple_of(i * width, width), width)

    def k_copy(g):
        return copy(k_ref.at[:, lanes(g, HD)], kprev.at[:, lanes(g, HD)], k_s.at[g], k_r.at[g], {"seq": sq + 1})

    def v_copy(g):
        return copy(v_ref.at[:, lanes(g, HD)], vprev.at[:, lanes(g, HD)], v_s.at[g], v_r.at[g], {"seq": sq + 1})

    def hw_copy(p):
        return copy(hw_ref, hw_all.at[lanes(dp, FL), :], hw_s.at[p], hw_r.at[dp], {"dp": p})

    def hw_own(_):
        return copy(hw_ref, hw_all.at[lanes(dp, FL), :], hw_f.at[dp], hw_r.at[dp], {"dp": sib})

    def hw_pass(o):
        return copy(hw_all.at[lanes(o, FL), :], hw_all.at[lanes(o, FL), :], hw_f.at[o], hw_r.at[o], {"dp": sib})

    def vw_copy(p):
        return copy(vw_ref, vw_all.at[lanes(dp, 16), :], vw_s.at[p], vw_r.at[dp], {"dp": p})

    def vw_got(p):
        return copy(vw_ref, vw_all.at[lanes(p, 16), :], vw_s.at[p], vw_r.at[p], {"dp": p})

    def at_copy(o):
        return copy(att.at[:, lanes(o, FL)], shared.at[lanes(dp, BLOCK), :], at_s.at[o], at_r.at[dp], {"dp": o})

    def at_got(p):
        return copy(att.at[:, lanes(p, FL)], shared.at[lanes(p, BLOCK), :], at_s.at[p], at_r.at[p], {"dp": p})

    def st_copy(p):
        return copy(steer.at[lanes(dp, 8), :], steer.at[lanes(dp, 8), :], st_s.at[p], st_r.at[dp], {"dp": p})

    def st_got(p):
        return copy(steer.at[lanes(p, 8), :], steer.at[lanes(p, 8), :], st_s.at[p], st_r.at[p], {"dp": p})

    def vn_copy():
        return copy(v_out, v_in, vn_s.at[0], vn_r.at[0], {"seq": sq - 1})

    def dk_copy(g):
        return copy(dks.at[:, lanes(g, HD)], dkr.at[:, lanes(g, HD)], dk_s.at[g], dk_r.at[g], {"seq": sq - 1})

    def dv_copy(g):
        return copy(dvs.at[:, lanes(g, HD)], dvr.at[:, lanes(g, HD)], dv_s.at[g], dv_r.at[g], {"seq": sq - 1})

    def pre_copy(c):
        w = pl.ds(*cuts[c])
        return copy(pre_out.at[w, :], pre_in.at[w, :], pre_s.at[c], pre_r.at[c], {"seq": sq + 1})

    def suf_copy(c):
        w = pl.ds(*cuts[c])
        return copy(suf_out.at[w, :], suf_in.at[w, :], suf_s.at[c], suf_r.at[c], {"seq": sq - 1})

    def loop(low, high, body):
        def step(i, carry):
            body(i)
            return carry

        lax.fori_loop(low, high, step, 0)

    has_left, has_right = sq > 0, sq < S - 1

    barrier = pltpu.get_barrier_semaphore()

    @functools.partial(loop, 1, D)
    def _(m):
        pl.semaphore_signal(barrier, inc=1, device_id={"dp": (dp + m) % D}, device_id_type=MESH)

    @pl.when(has_left)
    def _():
        pl.semaphore_signal(barrier, inc=1, device_id={"seq": sq - 1}, device_id_type=MESH)

    @pl.when(has_right)
    def _():
        pl.semaphore_signal(barrier, inc=1, device_id={"seq": sq + 1}, device_id_type=MESH)

    pl.semaphore_wait(barrier, D - 1 + jnp.where(has_left, 1, 0) + jnp.where(has_right, 1, 0))

    @pl.when(has_right)
    def _():
        @functools.partial(loop, 0, KV_HEADS)
        def _(j):
            g = order(j)
            k_copy(g).start()
            v_copy(g).start()

    hw_own(0).start()

    @functools.partial(loop, 1, D // 2)
    def _(m):
        hw_copy((dp + D - 2 * m) % D).start()

    @functools.partial(loop, 1, D)
    def _(m):
        vw_copy((dp + m) % D).start()

    hw_all[lanes(dp, FL), :] = hw_ref[...]
    vw_all[lanes(dp, 16), :] = vw_ref[...]

    @pl.when(sq == 0)
    def _():
        kprev[...] = jnp.zeros_like(kprev)
        vprev[...] = jnp.zeros_like(vprev)
        pre_in[...] = jnp.zeros_like(pre_in)

    @pl.when(sq == S - 1)
    def _():
        dkr[...] = jnp.zeros_like(dkr)
        dvr[...] = jnp.zeros_like(dvr)
        v_in[...] = jnp.zeros_like(v_in)
        suf_in[...] = jnp.zeros_like(suf_in)

    mine = ep_ref[0, sq]
    left_ep = jnp.where(has_left, ep_ref[0, jnp.maximum(sq - 1, 0)], -1)
    right_ep = jnp.where(has_right, ep_ref[0, jnp.minimum(sq + 1, S - 1)], -1)
    key_at = lax.broadcasted_iota(jnp.int32, (BLOCK, BLOCK), 0)
    query_at = lax.broadcasted_iota(jnp.int32, (BLOCK, BLOCK), 1)
    mine_v = jnp.full((BLOCK, BLOCK), mine, jnp.int32)
    bias[:BLOCK, :] = jnp.where(mine_v == jnp.full((BLOCK, BLOCK), left_ep, jnp.int32), 0.0, NEG_FILL)
    bias[BLOCK:, :] = jnp.where(key_at <= query_at, 0.0, NEG_FILL)
    q_acc[...] = jnp.zeros_like(q_acc)
    v_acc[...] = jnp.zeros_like(v_acc)

    @functools.partial(loop, 1, D)
    def _(m):
        vw_got((dp + m) % D).wait_recv()

    def value_row(g):
        if R == 1:
            return vw_all[lanes(g, 16), :][0:1, :].astype(F32)
        return jnp.concatenate(
            [vw_all[lanes(g * R + r, 16), :][0:1, :].astype(F32) for r in range(R)], axis=1
        )

    def pair(prev, own, g):
        return jnp.concatenate([prev[:, lanes(g, HD)], own[:, lanes(g, HD)]], axis=0)

    @functools.partial(loop, 0, KV_HEADS)
    def _(j):
        g = order(j)

        @pl.when(has_left)
        def _():
            k_copy(g).wait_recv()
            v_copy(g).wait_recv()

        s = mul(pair(kprev, k_ref, g), stacked(q_ref[:, lanes(g, GW)]), NT) * SCALE
        s = s + jnp.concatenate([bias[...]] * GROUP, axis=1)
        e = jnp.exp(s - jnp.max(s, axis=0, keepdims=True))
        p = (e * (1.0 / jnp.sum(e, axis=0, keepdims=True))).astype(BF16)
        probs[g] = p
        a = side_by_side(mul(p, pair(vprev, v_ref, g), TN)).astype(BF16)
        att[:, lanes(g, GW)] = a
        for r in range(R):
            o = g * R + r

            @pl.when(o != dp)
            def _():
                at_copy(o).start()

            @pl.when(o == dp)
            def _():
                shared[lanes(dp, BLOCK), :] = att[:, lanes(o, FL)]

        for r in range(R):
            o = g * R + r

            @pl.when(jnp.logical_and(o != dp, o % 2 == dp % 2))
            def _():
                hw_pass(o).wait_recv()
                hw_pass(o).start()

        for r in range(R):
            o = g * R + r

            @pl.when(o % 2 != dp % 2)
            def _():
                hw_pass(o).wait_recv()

        q_acc[...] += mul(a, hw_all[lanes(g, GW), :], NN)
        weighed = a.astype(F32) * value_row(g)
        v_acc[...] += sum(weighed[:, i * HD : (i + 1) * HD] for i in range(GROUP))

    wide = (BLOCK, BLOCK)
    act_row = act_ref[...].astype(F32)
    act_b = jnp.broadcast_to(act_row, wide).T
    rew_b = jnp.broadcast_to(rew_ref[...].astype(F32), wide).T
    hot = jnp.concatenate([act_b, act_b], axis=1) == lax.broadcasted_iota(
        jnp.int32, (BLOCK, ACTS), 1
    ).astype(F32)
    v_now = jnp.broadcast_to(jnp.sum(v_acc[...], axis=1, keepdims=True), wide)
    v_out[...] = v_now[:8]

    @pl.when(has_left)
    def _():
        vn_copy().start()

    q_taken = jnp.broadcast_to(
        jnp.sum(jnp.where(hot, q_acc[...], 0.0), axis=1, keepdims=True), wide
    )

    @pl.when(has_right)
    def _():
        vn_copy().wait_recv()

    after = jnp.where(
        mine_v == jnp.full(wide, right_ep, jnp.int32), jnp.broadcast_to(v_in[0:1, :], wide), 0.0
    )
    v_next = jnp.where(key_at == BLOCK - 1, after, pltpu.roll(v_now, BLOCK - 1, 0))
    err = q_taken - (rew_b / REWARD_UNIT + GAMMA * v_next)
    gap = q_taken - v_now
    weight = jnp.where(gap < 0, 1.0 - TAU, TAU)
    grad_q = (2.0 * err).astype(BF16).astype(F32)
    grad_v = (-2.0 * weight * gap).astype(BF16).astype(F32)
    gvb[...] = grad_v
    sel[...] = jnp.where(hot, jnp.concatenate([grad_q, grad_q], axis=1), 0.0).astype(BF16)
    steer[lanes(dp, 8), :] = jnp.concatenate(
        [grad_q.T[0:1], grad_v.T[0:1], act_row, jnp.zeros((5, BLOCK), F32)], axis=0
    )

    @functools.partial(loop, 1, D)
    def _(m):
        st_copy((dp + m) % D).start()

    def backward(j):
        g = order(j)
        v_row = value_row(g)
        d = mul(sel[...], hw_all[lanes(g, GW), :], NT)
        d = (d + jnp.concatenate([gvb[...]] * GROUP, axis=1) * v_row).astype(BF16)
        d4 = stacked(d)
        p_low = probs[g]
        p = p_low.astype(F32)
        d_p = mul(pair(vprev, v_ref, g), d4, NT)
        delta = jnp.sum(p * d_p, axis=0, keepdims=True)
        d_s = (p * (d_p - delta) * SCALE).astype(BF16)
        dk = mul(d_s, stacked(q_ref[:, lanes(g, GW)]), NN)
        dv = mul(p_low, d4, NN)
        dks[:, lanes(g, HD)] = dk[:BLOCK].astype(BF16)
        dvs[:, lanes(g, HD)] = dv[:BLOCK].astype(BF16)

        @pl.when(has_left)
        def _():
            dk_copy(g).start()
            dv_copy(g).start()

        dka[:, lanes(g, HD)] = dk[BLOCK:]
        dva[:, lanes(g, HD)] = dv[BLOCK:]
        dq_ref[:, lanes(g, GW)] = side_by_side(mul(d_s, pair(kprev, k_ref, g), TN)).astype(BF16)

    def head_part():
        @functools.partial(loop, 1, D)
        def _(m):
            st_got((dp + m) % D).wait_recv()
            at_got((dp + m) % D).wait_recv()

        act_at = lax.broadcasted_iota(jnp.int32, (ACTS, BLOCK), 0).astype(F32)
        for r in range(D):
            w = pl.ds(r * BLOCK, BLOCK)
            one = steer[pl.ds(r * 8, 8), :]
            sel_t[:ACTS, w] = jnp.where(act_at == one[2:3], one[0:1], 0.0).astype(BF16)
            sel_t[ACTS:, w] = jnp.broadcast_to(one[1:2], (16, BLOCK)).astype(BF16)
        part[...] = mul(sel_t[...], shared[...], NN)

    def stage(k):
        @pl.when(sq == k)
        def _():
            for c, (low, size) in enumerate(cuts):
                if k > 0:
                    pre_copy(c).wait_recv()
                w = pl.ds(low, size)
                pre_out[w, :] = (part[w, :] + pre_in[w, :].astype(F32)).astype(BF16)
                pre_copy(c).start()

        @pl.when(sq == S - 1 - k)
        def _():
            for c, (low, size) in enumerate(cuts):
                if k > 0:
                    suf_copy(c).wait_recv()
                w = pl.ds(low, size)
                suf_out[w, :] = (part[w, :] + suf_in[w, :].astype(F32)).astype(BF16)
                suf_copy(c).start()

    for half in range(4):
        loop(2 * half, 2 * half + 2, backward)
        if half == 0:
            head_part()
        if half < S - 1:
            stage(half)
    for k in range(4, S - 1):
        stage(k)

    @functools.partial(loop, 0, KV_HEADS)
    def _(j):
        g = order(j)

        @pl.when(has_right)
        def _():
            dk_copy(g).wait_recv()
            dv_copy(g).wait_recv()

        w = lanes(g, HD)
        dk_ref[:, w] = (dka[:, w] + dkr[:, w].astype(F32)).astype(BF16)
        dv_ref[:, w] = (dva[:, w] + dvr[:, w].astype(F32)).astype(BF16)

    @pl.when(sq == S - 1)
    def _():
        for c in range(len(cuts)):
            pre_copy(c).wait_recv()

    @pl.when(sq == 0)
    def _():
        for c in range(len(cuts)):
            suf_copy(c).wait_recv()

    total = part[...] + pre_in[...].astype(F32) + suf_in[...].astype(F32)
    gh_ref[...] = total[:ACTS].T
    gv_ref[...] = total[ACTS : ACTS + 8]

    @pl.when(has_right)
    def _():
        @functools.partial(loop, 0, KV_HEADS)
        def _(g):
            k_copy(g).wait_send()
            v_copy(g).wait_send()

        for c in range(len(cuts)):
            pre_copy(c).wait_send()

    @pl.when(has_left)
    def _():
        @functools.partial(loop, 0, KV_HEADS)
        def _(g):
            dk_copy(g).wait_send()
            dv_copy(g).wait_send()

        vn_copy().wait_send()
        for c in range(len(cuts)):
            suf_copy(c).wait_send()

    hw_own(0).wait_send()

    @functools.partial(loop, 1, D // 2)
    def _(m):
        hw_copy((dp + D - 2 * m) % D).wait_send()
        hw_pass((dp + 2 * m) % D).wait_send()

    @functools.partial(loop, 1, D)
    def _(m):
        p = (dp + m) % D
        vw_copy(p).wait_send()
        at_copy(p).wait_send()
        st_copy(p).wait_send()


def per_device(D, S, queries, keys, values, head_weight, value_weight, action_ids, rewards, episode_ids):
    FL = head_weight.shape[0]
    qw, kw = HEADS * HD, KV_HEADS * HD
    rows = ACTS + 16
    dma = lambda n: pltpu.SemaphoreType.DMA((n,))
    vm = pltpu.VMEM
    vmem = pl.BlockSpec(memory_space=pltpu.VMEM)
    values_row = jnp.broadcast_to(value_weight[None], (16, FL))
    outs = pl.pallas_call(
        functools.partial(kernel, D, S, FL),
        out_shape=(
            jax.ShapeDtypeStruct((BLOCK, qw), BF16),
            jax.ShapeDtypeStruct((BLOCK, kw), BF16),
            jax.ShapeDtypeStruct((BLOCK, kw), BF16),
            jax.ShapeDtypeStruct((FL, ACTS), F32),
            jax.ShapeDtypeStruct((8, FL), F32),
        ),
        in_specs=[vmem] * 7 + [pl.BlockSpec(memory_space=pltpu.SMEM)],
        out_specs=(vmem,) * 5,
        scratch_shapes=[
            vm((BLOCK, kw), BF16), vm((BLOCK, kw), BF16),
            vm((qw, ACTS), BF16), vm((D * 16, FL), BF16),
            vm((2 * BLOCK, BLOCK), F32), vm((KV_HEADS, 2 * BLOCK, GW), BF16),
            vm((BLOCK, qw), BF16), vm((D * BLOCK, FL), BF16),
            vm((BLOCK, ACTS), F32), vm((BLOCK, BLOCK), F32),
            vm((8, BLOCK), F32), vm((8, BLOCK), F32),
            vm((BLOCK, ACTS), BF16), vm((BLOCK, BLOCK), F32), vm((D * 8, BLOCK), F32),
            vm((rows, D * BLOCK), BF16),
            vm((BLOCK, kw), BF16), vm((BLOCK, kw), BF16),
            vm((BLOCK, kw), BF16), vm((BLOCK, kw), BF16),
            vm((BLOCK, kw), F32), vm((BLOCK, kw), F32),
            vm((rows, FL), F32),
            vm((rows, FL), BF16), vm((rows, FL), BF16), vm((rows, FL), BF16), vm((rows, FL), BF16),
            dma(KV_HEADS), dma(KV_HEADS), dma(KV_HEADS), dma(KV_HEADS),
            dma(D), dma(D), dma(D), dma(D), dma(D), dma(D), dma(D), dma(D), dma(D),
            dma(1), dma(1),
            dma(KV_HEADS), dma(KV_HEADS), dma(KV_HEADS), dma(KV_HEADS),
            dma(2), dma(2), dma(2), dma(2),
        ],
        compiler_params=pltpu.CompilerParams(
            collective_id=0, has_side_effects=True, vmem_limit_bytes=48 * 2**20
        ),
    )(queries[0], keys[0], values[0], head_weight, values_row, action_ids, rewards, episode_ids)
    dq, dk, dv, gh, gv = outs
    return (dq[None], dk[None], dv[None], gh, gv[0])


def solution(mesh):
    return jax.shard_map(
        functools.partial(per_device, mesh.shape["dp"], mesh.shape["seq"]),
        mesh=mesh,
        in_specs=(
            P("dp", "seq", None),
            P("dp", "seq", None),
            P("dp", "seq", None),
            P("dp", None),
            P("dp"),
            P("dp", "seq"),
            P("dp", "seq"),
            P("dp", None),
        ),
        out_specs=(
            P("dp", "seq", None),
            P("dp", "seq", None),
            P("dp", "seq", None),
            P("dp", None),
            P("dp"),
        ),
        check_vma=False,
    )
```

```python
import functools

import jax
import jax.numpy as jnp
from jax import lax
from jax.experimental import pallas as pl
from jax.experimental.pallas import tpu as pltpu
from jax.sharding import PartitionSpec as P

HEADS = 32
KV_HEADS = 8
HD = 128
ACTS = 256
BLOCK = 128
GROUP = HEADS // KV_HEADS
GW = GROUP * HD

GAMMA = 0.99
TAU = 0.7
REWARD_UNIT = 64.0
NEG_FILL = -1e30
SCALE = HD ** (-0.5)

F32 = jnp.float32
BF16 = jnp.bfloat16
MESH = pl.DeviceIdType.MESH

NT = (((1,), (1,)), ((), ()))
NN = (((1,), (0,)), ((), ()))
TN = (((0,), (0,)), ((), ()))


def mul(a, b, dims):
    return lax.dot_general(a, b, dims, preferred_element_type=F32)


def stacked(x):
    return jnp.concatenate([x[:, i * HD : (i + 1) * HD] for i in range(GROUP)], axis=0)


def side_by_side(x):
    return jnp.concatenate([x[i * BLOCK : (i + 1) * BLOCK] for i in range(GROUP)], axis=1)


def kernel(
    D, S, FL,
    q_hbm, k_hbm, v_hbm, hw_ref, vw_ref, act_ref, rew_ref, ep_ref,
    dq_ref, dk_ref, dv_ref, gh_ref, gv_ref,
    q_ref, k_ref, v_ref, in_sem, kprev, vprev, hw_all, vw_all, bias, probs, att, shared, q_acc, v_acc, v_out, v_in,
    sel, gvb, steer, sel_t, dks, dvs, dkr, dvr, dka, dva, part, pre_in, pre_out, suf_in, suf_out,
    k_s, k_r, v_s, v_r, hw_s, hw_f, hw_r, vw_s, vw_r, at_s, at_r, st_s, st_r, vn_s, vn_r,
    dk_s, dk_r, dv_s, dv_r, pre_s, pre_r, suf_s, suf_r,
):
    dp = lax.axis_index("dp")
    sq = lax.axis_index("seq")
    sib = dp + 1 - 2 * (dp % 2)
    R = GW // FL
    rows = ACTS + 16
    cuts = tuple((32 * c, 32) for c in range(7)) + ((224, rows - 224),)

    def copy(src, dst, ss, rs, where):
        return pltpu.make_async_remote_copy(
            src_ref=src, dst_ref=dst, send_sem=ss, recv_sem=rs, device_id=where, device_id_type=MESH
        )

    def order(j):
        if R == 1:
            return (dp + j - 2 * (dp % 2) * (j % 2) + D) % D
        return (dp // R + j) % KV_HEADS

    def lanes(i, width):
        return pl.ds(pl.multiple_of(i * width, width), width)

    def k_copy(g):
        return copy(k_hbm.at[:, lanes(g, HD)], kprev.at[g], k_s.at[g], k_r.at[g], {"seq": sq + 1})

    def v_copy(g):
        return copy(v_hbm.at[:, lanes(g, HD)], vprev.at[g], v_s.at[g], v_r.at[g], {"seq": sq + 1})

    def hw_copy(p):
        return copy(hw_ref, hw_all.at[lanes(dp, FL), :], hw_s.at[p], hw_r.at[dp], {"dp": p})

    def hw_own(_):
        return copy(hw_ref, hw_all.at[lanes(dp, FL), :], hw_f.at[dp], hw_r.at[dp], {"dp": sib})

    def hw_pass(o):
        return copy(hw_all.at[lanes(o, FL), :], hw_all.at[lanes(o, FL), :], hw_f.at[o], hw_r.at[o], {"dp": sib})

    def vw_copy(p):
        return copy(vw_ref, vw_all.at[lanes(dp, 16), :], vw_s.at[p], vw_r.at[dp], {"dp": p})

    def vw_got(p):
        return copy(vw_ref, vw_all.at[lanes(p, 16), :], vw_s.at[p], vw_r.at[p], {"dp": p})

    def at_copy(o):
        return copy(att.at[:, lanes(o, FL)], shared.at[lanes(dp, BLOCK), :], at_s.at[o], at_r.at[dp], {"dp": o})

    def at_got(p):
        return copy(att.at[:, lanes(p, FL)], shared.at[lanes(p, BLOCK), :], at_s.at[p], at_r.at[p], {"dp": p})

    def st_copy(p):
        return copy(steer.at[lanes(dp, 8), :], steer.at[lanes(dp, 8), :], st_s.at[p], st_r.at[dp], {"dp": p})

    def st_got(p):
        return copy(steer.at[lanes(p, 8), :], steer.at[lanes(p, 8), :], st_s.at[p], st_r.at[p], {"dp": p})

    def vn_copy():
        return copy(v_out, v_in, vn_s.at[0], vn_r.at[0], {"seq": sq - 1})

    def dk_copy(g):
        return copy(dks.at[g], dkr.at[g], dk_s.at[g], dk_r.at[g], {"seq": sq - 1})

    def dv_copy(g):
        return copy(dvs.at[g], dvr.at[g], dv_s.at[g], dv_r.at[g], {"seq": sq - 1})

    def pre_copy(c):
        w = pl.ds(*cuts[c])
        return copy(pre_out.at[w, :], pre_in.at[w, :], pre_s.at[c], pre_r.at[c], {"seq": sq + 1})

    def suf_copy(c):
        w = pl.ds(*cuts[c])
        return copy(suf_out.at[w, :], suf_in.at[w, :], suf_s.at[c], suf_r.at[c], {"seq": sq - 1})

    def loop(low, high, body):
        def step(i, carry):
            body(i)
            return carry

        lax.fori_loop(low, high, step, 0)

    has_left, has_right = sq > 0, sq < S - 1

    own = [
        pltpu.make_async_copy(k_hbm, k_ref, in_sem.at[0]),
        pltpu.make_async_copy(v_hbm, v_ref, in_sem.at[1]),
        pltpu.make_async_copy(q_hbm, q_ref, in_sem.at[2]),
        pltpu.make_async_copy(hw_ref, hw_all.at[lanes(dp, FL), :], in_sem.at[3]),
    ]

    barrier = pltpu.get_barrier_semaphore()

    @functools.partial(loop, 1, D)
    def _(m):
        pl.semaphore_signal(barrier, inc=1, device_id={"dp": (dp + m) % D}, device_id_type=MESH)

    @pl.when(has_left)
    def _():
        pl.semaphore_signal(barrier, inc=1, device_id={"seq": sq - 1}, device_id_type=MESH)

    @pl.when(has_right)
    def _():
        pl.semaphore_signal(barrier, inc=1, device_id={"seq": sq + 1}, device_id_type=MESH)

    pl.semaphore_wait(barrier, D - 1 + jnp.where(has_left, 1, 0) + jnp.where(has_right, 1, 0))

    @pl.when(has_right)
    def _():
        @functools.partial(loop, 0, KV_HEADS)
        def _(j):
            g = order(j)
            k_copy(g).start()
            v_copy(g).start()

    @functools.partial(loop, 1, D)
    def _(m):
        vw_copy((dp + m) % D).start()

    hw_own(0).start()

    @functools.partial(loop, 1, D // 2)
    def _(m):
        hw_copy((dp + D - 2 * m) % D).start()

    for one in own:
        one.start()
    vw_all[lanes(dp, 16), :] = vw_ref[...]

    @pl.when(sq == 0)
    def _():
        kprev[...] = jnp.zeros_like(kprev)
        vprev[...] = jnp.zeros_like(vprev)
        pre_in[...] = jnp.zeros_like(pre_in)

    @pl.when(sq == S - 1)
    def _():
        dkr[...] = jnp.zeros_like(dkr)
        dvr[...] = jnp.zeros_like(dvr)
        v_in[...] = jnp.zeros_like(v_in)
        suf_in[...] = jnp.zeros_like(suf_in)

    mine = ep_ref[0, sq]
    left_ep = jnp.where(has_left, ep_ref[0, jnp.maximum(sq - 1, 0)], -1)
    right_ep = jnp.where(has_right, ep_ref[0, jnp.minimum(sq + 1, S - 1)], -1)
    key_at = lax.broadcasted_iota(jnp.int32, (BLOCK, BLOCK), 0)
    query_at = lax.broadcasted_iota(jnp.int32, (BLOCK, BLOCK), 1)
    mine_v = jnp.full((BLOCK, BLOCK), mine, jnp.int32)
    bias[:BLOCK, :] = jnp.where(mine_v == jnp.full((BLOCK, BLOCK), left_ep, jnp.int32), 0.0, NEG_FILL)
    bias[BLOCK:, :] = jnp.where(key_at <= query_at, 0.0, NEG_FILL)
    for one in own:
        one.wait()
    q_acc[...] = jnp.zeros_like(q_acc)
    v_acc[...] = jnp.zeros_like(v_acc)

    @functools.partial(loop, 1, D)
    def _(m):
        vw_got((dp + m) % D).wait_recv()

    def pass_on(m):
        o = (dp + 2 * m) % D
        hw_pass(o).wait_recv()
        hw_pass(o).start()

    def value_row(g):
        if R == 1:
            return vw_all[lanes(g, 16), :][0:1, :].astype(F32)
        return jnp.concatenate(
            [vw_all[lanes(g * R + r, 16), :][0:1, :].astype(F32) for r in range(R)], axis=1
        )

    def pair(prev, own, g):
        return jnp.concatenate([prev[g], own[:, lanes(g, HD)]], axis=0)

    @functools.partial(loop, 0, KV_HEADS)
    def _(j):
        g = order(j)

        @pl.when(has_left)
        def _():
            k_copy(g).wait_recv()
            v_copy(g).wait_recv()

        s = mul(pair(kprev, k_ref, g), stacked(q_ref[:, lanes(g, GW)]), NT) * SCALE
        s = s + jnp.concatenate([bias[...]] * GROUP, axis=1)
        e = jnp.exp(s - jnp.max(s, axis=0, keepdims=True))
        p = (e * (1.0 / jnp.sum(e, axis=0, keepdims=True))).astype(BF16)
        probs[g] = p
        a = side_by_side(mul(p, pair(vprev, v_ref, g), TN)).astype(BF16)
        att[:, lanes(g, GW)] = a
        for r in range(R):
            o = g * R + r

            @pl.when(o != dp)
            def _():
                at_copy(o).start()

            @pl.when(o == dp)
            def _():
                shared[lanes(dp, BLOCK), :] = att[:, lanes(o, FL)]

        @pl.when(jnp.logical_and(j >= 5, j - 4 < D // 2))
        def _():
            pass_on(j - 4)

        weighed = a.astype(F32) * value_row(g)
        v_acc[...] += sum(weighed[:, i * HD : (i + 1) * HD] for i in range(GROUP))

    @functools.partial(loop, 4, D // 2)
    def _(m):
        pass_on(m)

    @functools.partial(loop, 0, KV_HEADS)
    def _(j):
        g = order(j)
        for r in range(R):
            o = g * R + r

            @pl.when(o % 2 != dp % 2)
            def _():
                hw_pass(o).wait_recv()

        q_acc[...] += mul(att[:, lanes(g, GW)], hw_all[lanes(g, GW), :], NN)

    wide = (BLOCK, BLOCK)
    act_row = act_ref[...].astype(F32)
    act_b = jnp.broadcast_to(act_row, wide).T
    rew_b = jnp.broadcast_to(rew_ref[...].astype(F32), wide).T
    hot = jnp.concatenate([act_b, act_b], axis=1) == lax.broadcasted_iota(
        jnp.int32, (BLOCK, ACTS), 1
    ).astype(F32)
    v_now = jnp.broadcast_to(jnp.sum(v_acc[...], axis=1, keepdims=True), wide)
    v_out[...] = v_now[:8]

    @pl.when(has_left)
    def _():
        vn_copy().start()

    q_taken = jnp.broadcast_to(
        jnp.sum(jnp.where(hot, q_acc[...], 0.0), axis=1, keepdims=True), wide
    )

    @pl.when(has_right)
    def _():
        vn_copy().wait_recv()

    after = jnp.where(
        mine_v == jnp.full(wide, right_ep, jnp.int32), jnp.broadcast_to(v_in[0:1, :], wide), 0.0
    )
    v_next = jnp.where(key_at == BLOCK - 1, after, pltpu.roll(v_now, BLOCK - 1, 0))
    err = q_taken - (rew_b / REWARD_UNIT + GAMMA * v_next)
    gap = q_taken - v_now
    weight = jnp.where(gap < 0, 1.0 - TAU, TAU)
    grad_q = (2.0 * err).astype(BF16).astype(F32)
    grad_v = (-2.0 * weight * gap).astype(BF16).astype(F32)
    gvb[...] = grad_v
    sel[...] = jnp.where(hot, jnp.concatenate([grad_q, grad_q], axis=1), 0.0).astype(BF16)
    steer[lanes(dp, 8), :] = jnp.concatenate(
        [grad_q.T[0:1], grad_v.T[0:1], act_row, jnp.zeros((5, BLOCK), F32)], axis=0
    )

    @functools.partial(loop, 1, D)
    def _(m):
        st_copy((dp + m) % D).start()

    def backward(j):
        g = order(j)
        v_row = value_row(g)
        d = mul(sel[...], hw_all[lanes(g, GW), :], NT)
        d = (d + jnp.concatenate([gvb[...]] * GROUP, axis=1) * v_row).astype(BF16)
        d4 = stacked(d)
        p_low = probs[g]
        p = p_low.astype(F32)
        d_p = mul(pair(vprev, v_ref, g), d4, NT)
        delta = jnp.sum(p * d_p, axis=0, keepdims=True)
        d_s = (p * (d_p - delta) * SCALE).astype(BF16)
        dk = mul(d_s, stacked(q_ref[:, lanes(g, GW)]), NN)
        dv = mul(p_low, d4, NN)
        dks[g] = dk[:BLOCK].astype(BF16)
        dvs[g] = dv[:BLOCK].astype(BF16)

        @pl.when(has_left)
        def _():
            dk_copy(g).start()
            dv_copy(g).start()

        dka[:, lanes(g, HD)] = dk[BLOCK:]
        dva[:, lanes(g, HD)] = dv[BLOCK:]
        dq_ref[:, lanes(g, GW)] = side_by_side(mul(d_s, pair(kprev, k_ref, g), TN)).astype(BF16)

    def head_part():
        @functools.partial(loop, 1, D)
        def _(m):
            st_got((dp + m) % D).wait_recv()
            at_got((dp + m) % D).wait_recv()

        act_at = lax.broadcasted_iota(jnp.int32, (ACTS, BLOCK), 0).astype(F32)
        for r in range(D):
            w = pl.ds(r * BLOCK, BLOCK)
            one = steer[pl.ds(r * 8, 8), :]
            sel_t[:ACTS, w] = jnp.where(act_at == one[2:3], one[0:1], 0.0).astype(BF16)
            sel_t[ACTS:, w] = jnp.broadcast_to(one[1:2], (16, BLOCK)).astype(BF16)
        part[...] = mul(sel_t[...], shared[...], NN)

    def pre_on(c):
        w = pl.ds(*cuts[c])
        pre_out[w, :] = (part[w, :] + pre_in[w, :].astype(F32)).astype(BF16)
        pre_copy(c).start()

    def suf_on(c):
        w = pl.ds(*cuts[c])
        suf_out[w, :] = (part[w, :] + suf_in[w, :].astype(F32)).astype(BF16)
        suf_copy(c).start()

    def ends():
        @pl.when(sq == 0)
        def _():
            for c in range(len(cuts)):
                pre_on(c)

        @pl.when(sq == S - 1)
        def _():
            for c in range(len(cuts)):
                suf_on(c)

    def middle(low, high):
        @pl.when(jnp.logical_and(has_left, has_right))
        def _():
            for c in range(low, high):
                pre_copy(c).wait_recv()
                pre_on(c)
                suf_copy(c).wait_recv()
                suf_on(c)

    loop(0, 2, backward)
    head_part()
    ends()
    loop(2, 4, backward)
    middle(0, 2)
    loop(4, 6, backward)
    middle(2, 5)
    loop(6, KV_HEADS, backward)
    middle(5, len(cuts))

    @functools.partial(loop, 0, KV_HEADS)
    def _(j):
        g = order(j)

        @pl.when(has_right)
        def _():
            dk_copy(g).wait_recv()
            dv_copy(g).wait_recv()

        w = lanes(g, HD)
        dk_ref[:, w] = (dka[:, w] + dkr[g].astype(F32)).astype(BF16)
        dv_ref[:, w] = (dva[:, w] + dvr[g].astype(F32)).astype(BF16)

    @pl.when(sq == S - 1)
    def _():
        for c in range(len(cuts)):
            pre_copy(c).wait_recv()

    @pl.when(sq == 0)
    def _():
        for c in range(len(cuts)):
            suf_copy(c).wait_recv()

    total = part[...] + pre_in[...].astype(F32) + suf_in[...].astype(F32)
    gh_ref[...] = total[:ACTS].T
    gv_ref[...] = total[ACTS : ACTS + 1]

    @pl.when(has_right)
    def _():
        @functools.partial(loop, 0, KV_HEADS)
        def _(g):
            k_copy(g).wait_send()
            v_copy(g).wait_send()

        for c in range(len(cuts)):
            pre_copy(c).wait_send()

    @pl.when(has_left)
    def _():
        @functools.partial(loop, 0, KV_HEADS)
        def _(g):
            dk_copy(g).wait_send()
            dv_copy(g).wait_send()

        vn_copy().wait_send()
        for c in range(len(cuts)):
            suf_copy(c).wait_send()

    hw_own(0).wait_send()

    @functools.partial(loop, 1, D // 2)
    def _(m):
        hw_copy((dp + D - 2 * m) % D).wait_send()
        hw_pass((dp + 2 * m) % D).wait_send()

    @functools.partial(loop, 1, D)
    def _(m):
        p = (dp + m) % D
        vw_copy(p).wait_send()
        at_copy(p).wait_send()
        st_copy(p).wait_send()


def per_device(D, S, queries, keys, values, head_weight, value_weight, action_ids, rewards, episode_ids):
    FL = head_weight.shape[0]
    qw, kw = HEADS * HD, KV_HEADS * HD
    rows = ACTS + 16
    dma = lambda n: pltpu.SemaphoreType.DMA((n,))
    vm = pltpu.VMEM
    halo = vm((KV_HEADS, BLOCK, HD), BF16)
    vmem = pl.BlockSpec(memory_space=pltpu.VMEM)
    values_row = jnp.broadcast_to(value_weight[None], (16, FL))
    outs = pl.pallas_call(
        functools.partial(kernel, D, S, FL),
        out_shape=(
            jax.ShapeDtypeStruct((BLOCK, qw), BF16),
            jax.ShapeDtypeStruct((BLOCK, kw), BF16),
            jax.ShapeDtypeStruct((BLOCK, kw), BF16),
            jax.ShapeDtypeStruct((FL, ACTS), F32),
            jax.ShapeDtypeStruct((1, FL), F32),
        ),
        in_specs=[pl.BlockSpec(memory_space=pl.ANY)] * 4 + [vmem] * 3 + [pl.BlockSpec(memory_space=pltpu.SMEM)],
        out_specs=(vmem,) * 5,
        scratch_shapes=[
            vm((BLOCK, qw), BF16), vm((BLOCK, kw), BF16), vm((BLOCK, kw), BF16), dma(4),
            halo, halo,
            vm((qw, ACTS), BF16), vm((D * 16, FL), BF16),
            vm((2 * BLOCK, BLOCK), F32), vm((KV_HEADS, 2 * BLOCK, GW), BF16),
            vm((BLOCK, qw), BF16), vm((D * BLOCK, FL), BF16),
            vm((BLOCK, ACTS), F32), vm((BLOCK, BLOCK), F32),
            vm((8, BLOCK), F32), vm((8, BLOCK), F32),
            vm((BLOCK, ACTS), BF16), vm((BLOCK, BLOCK), F32), vm((D * 8, BLOCK), F32),
            vm((rows, D * BLOCK), BF16),
            halo, halo, halo, halo,
            vm((BLOCK, kw), F32), vm((BLOCK, kw), F32),
            vm((rows, FL), F32),
            vm((rows, FL), BF16), vm((rows, FL), BF16), vm((rows, FL), BF16), vm((rows, FL), BF16),
            dma(KV_HEADS), dma(KV_HEADS), dma(KV_HEADS), dma(KV_HEADS),
            dma(D), dma(D), dma(D), dma(D), dma(D), dma(D), dma(D), dma(D), dma(D),
            dma(1), dma(1),
            dma(KV_HEADS), dma(KV_HEADS), dma(KV_HEADS), dma(KV_HEADS),
            dma(8), dma(8), dma(8), dma(8),
        ],
        compiler_params=pltpu.CompilerParams(
            collective_id=0, has_side_effects=True, vmem_limit_bytes=60 * 2**20
        ),
    )(queries[0], keys[0], values[0], head_weight, values_row, action_ids, rewards, episode_ids)
    dq, dk, dv, gh, gv = outs
    return (dq[None], dk[None], dv[None], gh, gv.reshape(FL))


def solution(mesh):
    return jax.shard_map(
        functools.partial(per_device, mesh.shape["dp"], mesh.shape["seq"]),
        mesh=mesh,
        in_specs=(
            P("dp", "seq", None),
            P("dp", "seq", None),
            P("dp", "seq", None),
            P("dp", None),
            P("dp"),
            P("dp", "seq"),
            P("dp", "seq"),
            P("dp", None),
        ),
        out_specs=(
            P("dp", "seq", None),
            P("dp", "seq", None),
            P("dp", "seq", None),
            P("dp", None),
            P("dp"),
        ),
        check_vma=False,
    )
```

```python
import functools

import jax
import jax.numpy as jnp
from jax import lax
from jax.experimental import pallas as pl
from jax.experimental.pallas import tpu as pltpu
from jax.sharding import PartitionSpec as P

HEADS = 32
KV_HEADS = 8
HD = 128
ACTS = 256
BLOCK = 128
GROUP = HEADS // KV_HEADS
GW = GROUP * HD

GAMMA = 0.99
TAU = 0.7
REWARD_UNIT = 64.0
NEG_FILL = -1e30
SCALE = HD ** (-0.5)

F32 = jnp.float32
BF16 = jnp.bfloat16
MESH = pl.DeviceIdType.MESH

NT = (((1,), (1,)), ((), ()))
NN = (((1,), (0,)), ((), ()))
TN = (((0,), (0,)), ((), ()))


def mul(a, b, dims):
    return lax.dot_general(a, b, dims, preferred_element_type=F32)


def stacked(x):
    return jnp.concatenate([x[:, i * HD : (i + 1) * HD] for i in range(GROUP)], axis=0)


def side_by_side(x):
    return jnp.concatenate([x[i * BLOCK : (i + 1) * BLOCK] for i in range(GROUP)], axis=1)


def kernel(
    D, S, FL,
    q_hbm, k_hbm, v_hbm, hw_ref, vw_ref, act_ref, rew_ref, ep_ref,
    dq_ref, dk_ref, dv_ref, gh_ref, gv_ref,
    q_ref, k_ref, v_ref, in_sem, kprev, vprev, hw_all, vw_all, bias, probs, att, shared, q_acc, v_acc, v_out, v_in,
    sel, gvb, steer, sel_t, dks, dvs, dkr, dvr, dka, dva, part, pre_in, pre_out, suf_in, suf_out,
    k_s, k_r, v_s, v_r, hw_s, hw_f, hw_r, vw_s, vw_r, at_s, at_r, st_s, st_r, vn_s, vn_r,
    dk_s, dk_r, dv_s, dv_r, pre_s, pre_r, suf_s, suf_r,
):
    dp = lax.axis_index("dp")
    sq = lax.axis_index("seq")
    sib = dp + 1 - 2 * (dp % 2)
    R = GW // FL
    rows = ACTS + 16
    cuts = ((0, 64), (64, 64), (128, 64), (192, rows - 192))

    def copy(src, dst, ss, rs, where):
        return pltpu.make_async_remote_copy(
            src_ref=src, dst_ref=dst, send_sem=ss, recv_sem=rs, device_id=where, device_id_type=MESH
        )

    def order(j):
        if R == 1:
            return (dp + j - 2 * (dp % 2) * (j % 2) + D) % D
        return (dp // R + j) % KV_HEADS

    def lanes(i, width):
        return pl.ds(pl.multiple_of(i * width, width), width)

    def k_copy(g):
        return copy(k_hbm.at[:, lanes(g, HD)], kprev.at[g], k_s.at[g], k_r.at[g], {"seq": sq + 1})

    def v_copy(g):
        return copy(v_hbm.at[:, lanes(g, HD)], vprev.at[g], v_s.at[g], v_r.at[g], {"seq": sq + 1})

    def hw_copy(p):
        return copy(hw_ref, hw_all.at[lanes(dp, FL), :], hw_s.at[p], hw_r.at[dp], {"dp": p})

    def hw_own(_):
        return copy(hw_ref, hw_all.at[lanes(dp, FL), :], hw_f.at[dp], hw_r.at[dp], {"dp": sib})

    def hw_pass(o):
        return copy(hw_all.at[lanes(o, FL), :], hw_all.at[lanes(o, FL), :], hw_f.at[o], hw_r.at[o], {"dp": sib})

    def vw_copy(p):
        return copy(vw_ref, vw_all.at[lanes(dp, 16), :], vw_s.at[p], vw_r.at[dp], {"dp": p})

    def vw_got(p):
        return copy(vw_ref, vw_all.at[lanes(p, 16), :], vw_s.at[p], vw_r.at[p], {"dp": p})

    def at_copy(o):
        return copy(att.at[:, lanes(o, FL)], shared.at[lanes(dp, BLOCK), :], at_s.at[o], at_r.at[dp], {"dp": o})

    def at_got(p):
        return copy(att.at[:, lanes(p, FL)], shared.at[lanes(p, BLOCK), :], at_s.at[p], at_r.at[p], {"dp": p})

    def st_copy(p):
        return copy(steer.at[lanes(dp, 8), :], steer.at[lanes(dp, 8), :], st_s.at[p], st_r.at[dp], {"dp": p})

    def st_got(p):
        return copy(steer.at[lanes(p, 8), :], steer.at[lanes(p, 8), :], st_s.at[p], st_r.at[p], {"dp": p})

    def vn_copy():
        return copy(v_out, v_in, vn_s.at[0], vn_r.at[0], {"seq": sq - 1})

    def dk_copy(g):
        return copy(dks.at[g], dkr.at[g], dk_s.at[g], dk_r.at[g], {"seq": sq - 1})

    def dv_copy(g):
        return copy(dvs.at[g], dvr.at[g], dv_s.at[g], dv_r.at[g], {"seq": sq - 1})

    def pre_copy(c):
        w = pl.ds(*cuts[c])
        return copy(pre_out.at[w, :], pre_in.at[w, :], pre_s.at[c], pre_r.at[c], {"seq": sq + 1})

    def suf_copy(c):
        w = pl.ds(*cuts[c])
        return copy(suf_out.at[w, :], suf_in.at[w, :], suf_s.at[c], suf_r.at[c], {"seq": sq - 1})

    def loop(low, high, body):
        def step(i, carry):
            body(i)
            return carry

        lax.fori_loop(low, high, step, 0)

    has_left, has_right = sq > 0, sq < S - 1

    own = [
        pltpu.make_async_copy(k_hbm, k_ref, in_sem.at[0]),
        pltpu.make_async_copy(v_hbm, v_ref, in_sem.at[1]),
        pltpu.make_async_copy(q_hbm, q_ref, in_sem.at[2]),
        pltpu.make_async_copy(hw_ref, hw_all.at[lanes(dp, FL), :], in_sem.at[3]),
    ]

    barrier = pltpu.get_barrier_semaphore()

    @functools.partial(loop, 1, D)
    def _(m):
        pl.semaphore_signal(barrier, inc=1, device_id={"dp": (dp + m) % D}, device_id_type=MESH)

    @pl.when(has_left)
    def _():
        pl.semaphore_signal(barrier, inc=1, device_id={"seq": sq - 1}, device_id_type=MESH)

    @pl.when(has_right)
    def _():
        pl.semaphore_signal(barrier, inc=1, device_id={"seq": sq + 1}, device_id_type=MESH)

    pl.semaphore_wait(barrier, D - 1 + jnp.where(has_left, 1, 0) + jnp.where(has_right, 1, 0))

    @pl.when(has_right)
    def _():
        @functools.partial(loop, 0, KV_HEADS)
        def _(j):
            g = order(j)
            k_copy(g).start()
            v_copy(g).start()

    @functools.partial(loop, 1, D)
    def _(m):
        vw_copy((dp + m) % D).start()

    hw_own(0).start()

    @functools.partial(loop, 1, D // 2)
    def _(m):
        hw_copy((dp + D - 2 * m) % D).start()

    for one in own:
        one.start()
    vw_all[lanes(dp, 16), :] = vw_ref[...]

    @pl.when(sq == 0)
    def _():
        kprev[...] = jnp.zeros_like(kprev)
        vprev[...] = jnp.zeros_like(vprev)
        pre_in[...] = jnp.zeros_like(pre_in)

    @pl.when(sq == S - 1)
    def _():
        dkr[...] = jnp.zeros_like(dkr)
        dvr[...] = jnp.zeros_like(dvr)
        v_in[...] = jnp.zeros_like(v_in)
        suf_in[...] = jnp.zeros_like(suf_in)

    mine = ep_ref[0, sq]
    left_ep = jnp.where(has_left, ep_ref[0, jnp.maximum(sq - 1, 0)], -1)
    right_ep = jnp.where(has_right, ep_ref[0, jnp.minimum(sq + 1, S - 1)], -1)
    key_at = lax.broadcasted_iota(jnp.int32, (BLOCK, BLOCK), 0)
    query_at = lax.broadcasted_iota(jnp.int32, (BLOCK, BLOCK), 1)
    mine_v = jnp.full((BLOCK, BLOCK), mine, jnp.int32)
    bias[:BLOCK, :] = jnp.where(mine_v == jnp.full((BLOCK, BLOCK), left_ep, jnp.int32), 0.0, NEG_FILL)
    bias[BLOCK:, :] = jnp.where(key_at <= query_at, 0.0, NEG_FILL)
    for one in own:
        one.wait()
    q_acc[...] = jnp.zeros_like(q_acc)
    v_acc[...] = jnp.zeros_like(v_acc)

    @functools.partial(loop, 1, D)
    def _(m):
        vw_got((dp + m) % D).wait_recv()

    def pass_on(m):
        o = (dp + 2 * m) % D
        hw_pass(o).wait_recv()
        hw_pass(o).start()

    def value_row(g):
        if R == 1:
            return vw_all[lanes(g, 16), :][0:1, :].astype(F32)
        return jnp.concatenate(
            [vw_all[lanes(g * R + r, 16), :][0:1, :].astype(F32) for r in range(R)], axis=1
        )

    def pair(prev, own, g):
        return jnp.concatenate([prev[g], own[:, lanes(g, HD)]], axis=0)

    @functools.partial(loop, 0, KV_HEADS)
    def _(j):
        g = order(j)

        @pl.when(has_left)
        def _():
            k_copy(g).wait_recv()
            v_copy(g).wait_recv()

        s = mul(pair(kprev, k_ref, g), stacked(q_ref[:, lanes(g, GW)]), NT) * SCALE
        s = s + jnp.concatenate([bias[...]] * GROUP, axis=1)
        e = jnp.exp(s - jnp.max(s, axis=0, keepdims=True))
        p = (e * (1.0 / jnp.sum(e, axis=0, keepdims=True))).astype(BF16)
        probs[g] = p
        a = side_by_side(mul(p, pair(vprev, v_ref, g), TN)).astype(BF16)
        att[:, lanes(g, GW)] = a
        for r in range(R):
            o = g * R + r

            @pl.when(o != dp)
            def _():
                at_copy(o).start()

            @pl.when(o == dp)
            def _():
                shared[lanes(dp, BLOCK), :] = att[:, lanes(o, FL)]

        @pl.when(jnp.logical_and(j >= 5, j - 4 < D // 2))
        def _():
            pass_on(j - 4)

        weighed = a.astype(F32) * value_row(g)
        v_acc[...] += sum(weighed[:, i * HD : (i + 1) * HD] for i in range(GROUP))

    @functools.partial(loop, 4, D // 2)
    def _(m):
        pass_on(m)

    @functools.partial(loop, 0, KV_HEADS)
    def _(j):
        g = order(j)
        for r in range(R):
            o = g * R + r

            @pl.when(o % 2 != dp % 2)
            def _():
                hw_pass(o).wait_recv()

        q_acc[...] += mul(att[:, lanes(g, GW)], hw_all[lanes(g, GW), :], NN)

    wide = (BLOCK, BLOCK)
    act_row = act_ref[...].astype(F32)
    act_b = jnp.broadcast_to(act_row, wide).T
    rew_b = jnp.broadcast_to(rew_ref[...].astype(F32), wide).T
    hot = jnp.concatenate([act_b, act_b], axis=1) == lax.broadcasted_iota(
        jnp.int32, (BLOCK, ACTS), 1
    ).astype(F32)
    v_now = jnp.broadcast_to(jnp.sum(v_acc[...], axis=1, keepdims=True), wide)
    v_out[...] = v_now[:8]

    @pl.when(has_left)
    def _():
        vn_copy().start()

    q_taken = jnp.broadcast_to(
        jnp.sum(jnp.where(hot, q_acc[...], 0.0), axis=1, keepdims=True), wide
    )

    @pl.when(has_right)
    def _():
        vn_copy().wait_recv()

    after = jnp.where(
        mine_v == jnp.full(wide, right_ep, jnp.int32), jnp.broadcast_to(v_in[0:1, :], wide), 0.0
    )
    v_next = jnp.where(key_at == BLOCK - 1, after, pltpu.roll(v_now, BLOCK - 1, 0))
    err = q_taken - (rew_b / REWARD_UNIT + GAMMA * v_next)
    gap = q_taken - v_now
    weight = jnp.where(gap < 0, 1.0 - TAU, TAU)
    grad_q = (2.0 * err).astype(BF16).astype(F32)
    grad_v = (-2.0 * weight * gap).astype(BF16).astype(F32)
    gvb[...] = grad_v
    sel[...] = jnp.where(hot, jnp.concatenate([grad_q, grad_q], axis=1), 0.0).astype(BF16)
    steer[lanes(dp, 8), :] = jnp.concatenate(
        [grad_q.T[0:1], grad_v.T[0:1], act_row, jnp.zeros((5, BLOCK), F32)], axis=0
    )

    @functools.partial(loop, 1, D)
    def _(m):
        st_copy((dp + m) % D).start()

    def backward(j):
        g = order(j)
        v_row = value_row(g)
        d = mul(sel[...], hw_all[lanes(g, GW), :], NT)
        d = (d + jnp.concatenate([gvb[...]] * GROUP, axis=1) * v_row).astype(BF16)
        d4 = stacked(d)
        p_low = probs[g]
        p = p_low.astype(F32)
        d_p = mul(pair(vprev, v_ref, g), d4, NT)
        delta = jnp.sum(p * d_p, axis=0, keepdims=True)
        d_s = (p * (d_p - delta) * SCALE).astype(BF16)
        dk = mul(d_s, stacked(q_ref[:, lanes(g, GW)]), NN)
        dv = mul(p_low, d4, NN)
        dks[g] = dk[:BLOCK].astype(BF16)
        dvs[g] = dv[:BLOCK].astype(BF16)

        @pl.when(has_left)
        def _():
            dk_copy(g).start()
            dv_copy(g).start()

        dka[:, lanes(g, HD)] = dk[BLOCK:]
        dva[:, lanes(g, HD)] = dv[BLOCK:]
        dq_ref[:, lanes(g, GW)] = side_by_side(mul(d_s, pair(kprev, k_ref, g), TN)).astype(BF16)

    def head_part():
        @functools.partial(loop, 1, D)
        def _(m):
            st_got((dp + m) % D).wait_recv()
            at_got((dp + m) % D).wait_recv()

        act_at = lax.broadcasted_iota(jnp.int32, (ACTS, BLOCK), 0).astype(F32)
        for r in range(D):
            w = pl.ds(r * BLOCK, BLOCK)
            one = steer[pl.ds(r * 8, 8), :]
            sel_t[:ACTS, w] = jnp.where(act_at == one[2:3], one[0:1], 0.0).astype(BF16)
            sel_t[ACTS:, w] = jnp.broadcast_to(one[1:2], (16, BLOCK)).astype(BF16)
        part[...] = mul(sel_t[...], shared[...], NN)

    def pre_on(c):
        w = pl.ds(*cuts[c])
        pre_out[w, :] = (part[w, :] + pre_in[w, :].astype(F32)).astype(BF16)
        pre_copy(c).start()

    def suf_on(c):
        w = pl.ds(*cuts[c])
        suf_out[w, :] = (part[w, :] + suf_in[w, :].astype(F32)).astype(BF16)
        suf_copy(c).start()

    def ends():
        @pl.when(sq == 0)
        def _():
            for c in range(len(cuts)):
                pre_on(c)

        @pl.when(sq == S - 1)
        def _():
            for c in range(len(cuts)):
                suf_on(c)

    def pre_pass(low, high):
        for c in range(low, high):
            pre_copy(c).wait_recv()
            pre_on(c)

    def suf_pass(low, high):
        for c in range(low, high):
            suf_copy(c).wait_recv()
            suf_on(c)

    near_left = jnp.logical_and(has_left, sq < S // 2)
    near_right = jnp.logical_and(has_right, sq >= S // 2)

    def middle(low, high):
        @pl.when(near_left)
        def _():
            pre_pass(low, high)

        @pl.when(near_right)
        def _():
            suf_pass(low, high)

    def middle_far():
        @pl.when(near_left)
        def _():
            suf_pass(0, len(cuts))

        @pl.when(near_right)
        def _():
            pre_pass(0, len(cuts))

    loop(0, 2, backward)
    head_part()
    ends()
    loop(2, 6, backward)
    middle(0, 1)
    loop(6, KV_HEADS, backward)
    middle(1, len(cuts))
    middle_far()

    @functools.partial(loop, 0, KV_HEADS)
    def _(j):
        g = order(j)

        @pl.when(has_right)
        def _():
            dk_copy(g).wait_recv()
            dv_copy(g).wait_recv()

        w = lanes(g, HD)
        dk_ref[:, w] = (dka[:, w] + dkr[g].astype(F32)).astype(BF16)
        dv_ref[:, w] = (dva[:, w] + dvr[g].astype(F32)).astype(BF16)

    @pl.when(sq == S - 1)
    def _():
        for c in range(len(cuts)):
            pre_copy(c).wait_recv()

    @pl.when(sq == 0)
    def _():
        for c in range(len(cuts)):
            suf_copy(c).wait_recv()

    total = part[...] + pre_in[...].astype(F32) + suf_in[...].astype(F32)
    gh_ref[...] = total[:ACTS].T
    gv_ref[...] = total[ACTS : ACTS + 1]

    @pl.when(has_right)
    def _():
        @functools.partial(loop, 0, KV_HEADS)
        def _(g):
            k_copy(g).wait_send()
            v_copy(g).wait_send()

        for c in range(len(cuts)):
            pre_copy(c).wait_send()

    @pl.when(has_left)
    def _():
        @functools.partial(loop, 0, KV_HEADS)
        def _(g):
            dk_copy(g).wait_send()
            dv_copy(g).wait_send()

        vn_copy().wait_send()
        for c in range(len(cuts)):
            suf_copy(c).wait_send()

    hw_own(0).wait_send()

    @functools.partial(loop, 1, D // 2)
    def _(m):
        hw_copy((dp + D - 2 * m) % D).wait_send()
        hw_pass((dp + 2 * m) % D).wait_send()

    @functools.partial(loop, 1, D)
    def _(m):
        p = (dp + m) % D
        vw_copy(p).wait_send()
        at_copy(p).wait_send()
        st_copy(p).wait_send()


def per_device(D, S, queries, keys, values, head_weight, value_weight, action_ids, rewards, episode_ids):
    FL = head_weight.shape[0]
    qw, kw = HEADS * HD, KV_HEADS * HD
    rows = ACTS + 16
    dma = lambda n: pltpu.SemaphoreType.DMA((n,))
    vm = pltpu.VMEM
    halo = vm((KV_HEADS, BLOCK, HD), BF16)
    vmem = pl.BlockSpec(memory_space=pltpu.VMEM)
    values_row = jnp.broadcast_to(value_weight[None], (16, FL))
    outs = pl.pallas_call(
        functools.partial(kernel, D, S, FL),
        out_shape=(
            jax.ShapeDtypeStruct((BLOCK, qw), BF16),
            jax.ShapeDtypeStruct((BLOCK, kw), BF16),
            jax.ShapeDtypeStruct((BLOCK, kw), BF16),
            jax.ShapeDtypeStruct((FL, ACTS), F32),
            jax.ShapeDtypeStruct((1, FL), F32),
        ),
        in_specs=[pl.BlockSpec(memory_space=pl.ANY)] * 4 + [vmem] * 3 + [pl.BlockSpec(memory_space=pltpu.SMEM)],
        out_specs=(vmem,) * 5,
        scratch_shapes=[
            vm((BLOCK, qw), BF16), vm((BLOCK, kw), BF16), vm((BLOCK, kw), BF16), dma(4),
            halo, halo,
            vm((qw, ACTS), BF16), vm((D * 16, FL), BF16),
            vm((2 * BLOCK, BLOCK), F32), vm((KV_HEADS, 2 * BLOCK, GW), BF16),
            vm((BLOCK, qw), BF16), vm((D * BLOCK, FL), BF16),
            vm((BLOCK, ACTS), F32), vm((BLOCK, BLOCK), F32),
            vm((8, BLOCK), F32), vm((8, BLOCK), F32),
            vm((BLOCK, ACTS), BF16), vm((BLOCK, BLOCK), F32), vm((D * 8, BLOCK), F32),
            vm((rows, D * BLOCK), BF16),
            halo, halo, halo, halo,
            vm((BLOCK, kw), F32), vm((BLOCK, kw), F32),
            vm((rows, FL), F32),
            vm((rows, FL), BF16), vm((rows, FL), BF16), vm((rows, FL), BF16), vm((rows, FL), BF16),
            dma(KV_HEADS), dma(KV_HEADS), dma(KV_HEADS), dma(KV_HEADS),
            dma(D), dma(D), dma(D), dma(D), dma(D), dma(D), dma(D), dma(D), dma(D),
            dma(1), dma(1),
            dma(KV_HEADS), dma(KV_HEADS), dma(KV_HEADS), dma(KV_HEADS),
            dma(4), dma(4), dma(4), dma(4),
        ],
        compiler_params=pltpu.CompilerParams(
            collective_id=0, has_side_effects=True, vmem_limit_bytes=60 * 2**20
        ),
    )(queries[0], keys[0], values[0], head_weight, values_row, action_ids, rewards, episode_ids)
    dq, dk, dv, gh, gv = outs
    return (dq[None], dk[None], dv[None], gh, gv.reshape(FL))


def solution(mesh):
    return jax.shard_map(
        functools.partial(per_device, mesh.shape["dp"], mesh.shape["seq"]),
        mesh=mesh,
        in_specs=(
            P("dp", "seq", None),
            P("dp", "seq", None),
            P("dp", "seq", None),
            P("dp", None),
            P("dp"),
            P("dp", "seq"),
            P("dp", "seq"),
            P("dp", None),
        ),
        out_specs=(
            P("dp", "seq", None),
            P("dp", "seq", None),
            P("dp", "seq", None),
            P("dp", None),
            P("dp"),
        ),
        check_vma=False,
    )
```

```python
import functools

import jax
import jax.numpy as jnp
from jax import lax
from jax.experimental import pallas as pl
from jax.experimental.pallas import tpu as pltpu
from jax.sharding import PartitionSpec as P

HEADS = 32
KV_HEADS = 8
HD = 128
ACTS = 256
BLOCK = 128
GROUP = HEADS // KV_HEADS
GW = GROUP * HD

GAMMA = 0.99
TAU = 0.7
REWARD_UNIT = 64.0
NEG_FILL = -1e30
SCALE = HD ** (-0.5)

F32 = jnp.float32
BF16 = jnp.bfloat16
MESH = pl.DeviceIdType.MESH

NT = (((1,), (1,)), ((), ()))
NN = (((1,), (0,)), ((), ()))
TN = (((0,), (0,)), ((), ()))


def mul(a, b, dims):
    return lax.dot_general(a, b, dims, preferred_element_type=F32)


def stacked(x):
    return jnp.concatenate([x[:, i * HD : (i + 1) * HD] for i in range(GROUP)], axis=0)


def side_by_side(x):
    return jnp.concatenate([x[i * BLOCK : (i + 1) * BLOCK] for i in range(GROUP)], axis=1)


def kernel(
    D, S, FL,
    q_hbm, k_hbm, v_hbm, hw_ref, vw_ref, act_ref, rew_ref, ep_ref,
    dq_ref, dk_ref, dv_ref, gh_ref, gv_ref,
    q_ref, k_ref, v_ref, in_sem, kprev, vprev, hw_all, vw_all, bias, probs, att, shared, q_acc, v_acc, v_out, v_in,
    sel, gvb, steer, sel_t, dks, dvs, dkr, dvr, dka, dva, part, pre_in, pre_out, suf_in, suf_out,
    k_s, k_r, v_s, v_r, hw_s, hw_f, hw_r, vw_s, vw_r, at_s, at_r, st_s, st_r, vn_s, vn_r,
    dk_s, dk_r, dv_s, dv_r, pre_s, pre_r, suf_s, suf_r,
):
    dp = lax.axis_index("dp")
    sq = lax.axis_index("seq")
    sib = dp + 1 - 2 * (dp % 2)
    R = GW // FL
    rows = ACTS + 16
    cuts = ((0, 64), (64, 64), (128, 64), (192, rows - 192))

    def copy(src, dst, ss, rs, where):
        return pltpu.make_async_remote_copy(
            src_ref=src, dst_ref=dst, send_sem=ss, recv_sem=rs, device_id=where, device_id_type=MESH
        )

    def order(j):
        if R == 1:
            return (dp + j - 2 * (dp % 2) * (j % 2) + D) % D
        return (dp // R + j) % KV_HEADS

    def lanes(i, width):
        return pl.ds(pl.multiple_of(i * width, width), width)

    def k_copy(g):
        return copy(k_hbm.at[:, lanes(g, HD)], kprev.at[g], k_s.at[g], k_r.at[g], {"seq": sq + 1})

    def v_copy(g):
        return copy(v_hbm.at[:, lanes(g, HD)], vprev.at[g], v_s.at[g], v_r.at[g], {"seq": sq + 1})

    def hw_copy(p):
        return copy(hw_ref, hw_all.at[lanes(dp, FL), :], hw_s.at[p], hw_r.at[dp], {"dp": p})

    def hw_own(_):
        return copy(hw_ref, hw_all.at[lanes(dp, FL), :], hw_f.at[dp], hw_r.at[dp], {"dp": sib})

    def hw_pass(o):
        return copy(hw_all.at[lanes(o, FL), :], hw_all.at[lanes(o, FL), :], hw_f.at[o], hw_r.at[o], {"dp": sib})

    def vw_copy(p):
        return copy(vw_ref, vw_all.at[lanes(dp, 16), :], vw_s.at[p], vw_r.at[dp], {"dp": p})

    def vw_got(p):
        return copy(vw_ref, vw_all.at[lanes(p, 16), :], vw_s.at[p], vw_r.at[p], {"dp": p})

    def at_copy(o):
        return copy(att.at[:, lanes(o, FL)], shared.at[lanes(dp, BLOCK), :], at_s.at[o], at_r.at[dp], {"dp": o})

    def at_got(p):
        return copy(att.at[:, lanes(p, FL)], shared.at[lanes(p, BLOCK), :], at_s.at[p], at_r.at[p], {"dp": p})

    def st_copy(p):
        return copy(steer.at[lanes(dp, 8), :], steer.at[lanes(dp, 8), :], st_s.at[p], st_r.at[dp], {"dp": p})

    def st_got(p):
        return copy(steer.at[lanes(p, 8), :], steer.at[lanes(p, 8), :], st_s.at[p], st_r.at[p], {"dp": p})

    def vn_copy():
        return copy(v_out, v_in, vn_s.at[0], vn_r.at[0], {"seq": sq - 1})

    def dk_copy(g):
        return copy(dks.at[g], dkr.at[g], dk_s.at[g], dk_r.at[g], {"seq": sq - 1})

    def dv_copy(g):
        return copy(dvs.at[g], dvr.at[g], dv_s.at[g], dv_r.at[g], {"seq": sq - 1})

    def pre_copy(c):
        w = pl.ds(*cuts[c])
        return copy(pre_out.at[w, :], pre_in.at[w, :], pre_s.at[c], pre_r.at[c], {"seq": sq + 1})

    def suf_copy(c):
        w = pl.ds(*cuts[c])
        return copy(suf_out.at[w, :], suf_in.at[w, :], suf_s.at[c], suf_r.at[c], {"seq": sq - 1})

    def loop(low, high, body):
        def step(i, carry):
            body(i)
            return carry

        lax.fori_loop(low, high, step, 0)

    has_left, has_right = sq > 0, sq < S - 1

    own = [
        pltpu.make_async_copy(k_hbm, k_ref, in_sem.at[0]),
        pltpu.make_async_copy(v_hbm, v_ref, in_sem.at[1]),
        pltpu.make_async_copy(q_hbm, q_ref, in_sem.at[2]),
        pltpu.make_async_copy(hw_ref, hw_all.at[lanes(dp, FL), :], in_sem.at[3]),
    ]

    barrier = pltpu.get_barrier_semaphore()

    @functools.partial(loop, 1, D)
    def _(m):
        pl.semaphore_signal(barrier, inc=1, device_id={"dp": (dp + m) % D}, device_id_type=MESH)

    @pl.when(has_left)
    def _():
        pl.semaphore_signal(barrier, inc=1, device_id={"seq": sq - 1}, device_id_type=MESH)

    @pl.when(has_right)
    def _():
        pl.semaphore_signal(barrier, inc=1, device_id={"seq": sq + 1}, device_id_type=MESH)

    pl.semaphore_wait(barrier, D - 1 + jnp.where(has_left, 1, 0) + jnp.where(has_right, 1, 0))

    @pl.when(has_right)
    def _():
        @functools.partial(loop, 0, KV_HEADS)
        def _(j):
            g = order(j)
            k_copy(g).start()
            v_copy(g).start()

    @functools.partial(loop, 1, D)
    def _(m):
        vw_copy((dp + m) % D).start()

    hw_own(0).start()

    @functools.partial(loop, 1, D // 2)
    def _(m):
        hw_copy((dp + D - 2 * m) % D).start()

    for one in own:
        one.start()
    vw_all[lanes(dp, 16), :] = vw_ref[...]

    @pl.when(sq == 0)
    def _():
        kprev[...] = jnp.zeros_like(kprev)
        vprev[...] = jnp.zeros_like(vprev)
        pre_in[...] = jnp.zeros_like(pre_in)

    @pl.when(sq == S - 1)
    def _():
        dkr[...] = jnp.zeros_like(dkr)
        dvr[...] = jnp.zeros_like(dvr)
        v_in[...] = jnp.zeros_like(v_in)
        suf_in[...] = jnp.zeros_like(suf_in)

    mine = ep_ref[0, sq]
    left_ep = jnp.where(has_left, ep_ref[0, jnp.maximum(sq - 1, 0)], -1)
    right_ep = jnp.where(has_right, ep_ref[0, jnp.minimum(sq + 1, S - 1)], -1)
    key_at = lax.broadcasted_iota(jnp.int32, (BLOCK, BLOCK), 0)
    query_at = lax.broadcasted_iota(jnp.int32, (BLOCK, BLOCK), 1)
    mine_v = jnp.full((BLOCK, BLOCK), mine, jnp.int32)
    bias[:BLOCK, :] = jnp.where(mine_v == jnp.full((BLOCK, BLOCK), left_ep, jnp.int32), 0.0, NEG_FILL)
    bias[BLOCK:, :] = jnp.where(key_at <= query_at, 0.0, NEG_FILL)
    for one in own:
        one.wait()
    q_acc[...] = jnp.zeros_like(q_acc)
    v_acc[...] = jnp.zeros_like(v_acc)

    @functools.partial(loop, 1, D)
    def _(m):
        vw_got((dp + m) % D).wait_recv()

    def pass_on(m):
        o = (dp + 2 * m) % D
        hw_pass(o).wait_recv()
        hw_pass(o).start()

    def value_row(g):
        if R == 1:
            return vw_all[lanes(g, 16), :][0:1, :].astype(F32)
        return jnp.concatenate(
            [vw_all[lanes(g * R + r, 16), :][0:1, :].astype(F32) for r in range(R)], axis=1
        )

    def pair(prev, own, g):
        return jnp.concatenate([prev[g], own[:, lanes(g, HD)]], axis=0)

    @functools.partial(loop, 0, KV_HEADS)
    def _(j):
        g = order(j)

        @pl.when(has_left)
        def _():
            k_copy(g).wait_recv()
            v_copy(g).wait_recv()

        s = mul(pair(kprev, k_ref, g), stacked(q_ref[:, lanes(g, GW)]), NT) * SCALE
        s = s + jnp.concatenate([bias[...]] * GROUP, axis=1)
        e = jnp.exp(s - jnp.max(s, axis=0, keepdims=True))
        p = (e * (1.0 / jnp.sum(e, axis=0, keepdims=True))).astype(BF16)
        probs[g] = p
        a = side_by_side(mul(p, pair(vprev, v_ref, g), TN)).astype(BF16)
        att[:, lanes(g, GW)] = a
        for r in range(R):
            o = g * R + r

            @pl.when(o != dp)
            def _():
                at_copy(o).start()

            @pl.when(o == dp)
            def _():
                shared[lanes(dp, BLOCK), :] = att[:, lanes(o, FL)]

        @pl.when(jnp.logical_and(j >= 5, j - 4 < D // 2))
        def _():
            pass_on(j - 4)

        weighed = a.astype(F32) * value_row(g)
        v_acc[...] += sum(weighed[:, i * HD : (i + 1) * HD] for i in range(GROUP))

    @functools.partial(loop, 4, D // 2)
    def _(m):
        pass_on(m)

    @functools.partial(loop, 0, KV_HEADS)
    def _(j):
        g = order(j)
        for r in range(R):
            o = g * R + r

            @pl.when(o % 2 != dp % 2)
            def _():
                hw_pass(o).wait_recv()

        q_acc[...] += mul(att[:, lanes(g, GW)], hw_all[lanes(g, GW), :], NN)

    wide = (BLOCK, BLOCK)
    act_row = act_ref[...].astype(F32)
    act_b = jnp.broadcast_to(act_row, wide).T
    rew_b = jnp.broadcast_to(rew_ref[...].astype(F32), wide).T
    hot = jnp.concatenate([act_b, act_b], axis=1) == lax.broadcasted_iota(
        jnp.int32, (BLOCK, ACTS), 1
    ).astype(F32)
    v_now = jnp.broadcast_to(jnp.sum(v_acc[...], axis=1, keepdims=True), wide)
    v_out[...] = v_now[:8]

    @pl.when(has_left)
    def _():
        vn_copy().start()

    q_taken = jnp.broadcast_to(
        jnp.sum(jnp.where(hot, q_acc[...], 0.0), axis=1, keepdims=True), wide
    )

    @pl.when(has_right)
    def _():
        vn_copy().wait_recv()

    after = jnp.where(
        mine_v == jnp.full(wide, right_ep, jnp.int32), jnp.broadcast_to(v_in[0:1, :], wide), 0.0
    )
    v_next = jnp.where(key_at == BLOCK - 1, after, pltpu.roll(v_now, BLOCK - 1, 0))
    err = q_taken - (rew_b / REWARD_UNIT + GAMMA * v_next)
    gap = q_taken - v_now
    weight = jnp.where(gap < 0, 1.0 - TAU, TAU)
    grad_q = (2.0 * err).astype(BF16).astype(F32)
    grad_v = (-2.0 * weight * gap).astype(BF16).astype(F32)
    gvb[...] = grad_v
    sel[...] = jnp.where(hot, jnp.concatenate([grad_q, grad_q], axis=1), 0.0).astype(BF16)
    steer[lanes(dp, 8), :] = jnp.concatenate(
        [grad_q.T[0:1], grad_v.T[0:1], act_row, jnp.zeros((5, BLOCK), F32)], axis=0
    )

    @functools.partial(loop, 1, D)
    def _(m):
        st_copy((dp + m) % D).start()

    def backward(j):
        g = order(j)
        v_row = value_row(g)
        d = mul(sel[...], hw_all[lanes(g, GW), :], NT)
        d = (d + jnp.concatenate([gvb[...]] * GROUP, axis=1) * v_row).astype(BF16)
        d4 = stacked(d)
        p_low = probs[g]
        p = p_low.astype(F32)
        d_p = mul(pair(vprev, v_ref, g), d4, NT)
        delta = jnp.sum(p * d_p, axis=0, keepdims=True)
        d_s = (p * (d_p - delta) * SCALE).astype(BF16)
        dk = mul(d_s, stacked(q_ref[:, lanes(g, GW)]), NN)
        dv = mul(p_low, d4, NN)
        dks[g] = dk[:BLOCK].astype(BF16)
        dvs[g] = dv[:BLOCK].astype(BF16)

        @pl.when(has_left)
        def _():
            dk_copy(g).start()
            dv_copy(g).start()

        dka[:, lanes(g, HD)] = dk[BLOCK:]
        dva[:, lanes(g, HD)] = dv[BLOCK:]
        dq_ref[:, lanes(g, GW)] = side_by_side(mul(d_s, pair(kprev, k_ref, g), TN)).astype(BF16)

    def head_part():
        @functools.partial(loop, 1, D)
        def _(m):
            st_got((dp + m) % D).wait_recv()
            at_got((dp + m) % D).wait_recv()

        act_at = lax.broadcasted_iota(jnp.int32, (ACTS, BLOCK), 0).astype(F32)
        for r in range(D):
            w = pl.ds(r * BLOCK, BLOCK)
            one = steer[pl.ds(r * 8, 8), :]
            sel_t[:ACTS, w] = jnp.where(act_at == one[2:3], one[0:1], 0.0).astype(BF16)
            sel_t[ACTS:, w] = jnp.broadcast_to(one[1:2], (16, BLOCK)).astype(BF16)
        part[...] = mul(sel_t[...], shared[...], NN)

    def pre_on(c):
        w = pl.ds(*cuts[c])
        pre_out[w, :] = (part[w, :] + pre_in[w, :].astype(F32)).astype(BF16)
        pre_copy(c).start()

    def suf_on(c):
        w = pl.ds(*cuts[c])
        suf_out[w, :] = (part[w, :] + suf_in[w, :].astype(F32)).astype(BF16)
        suf_copy(c).start()

    def ends():
        @pl.when(sq == 0)
        def _():
            for c in range(len(cuts)):
                pre_on(c)

        @pl.when(sq == S - 1)
        def _():
            for c in range(len(cuts)):
                suf_on(c)

    def pre_pass(low, high):
        for c in range(low, high):
            pre_copy(c).wait_recv()
            pre_on(c)

    def suf_pass(low, high):
        for c in range(low, high):
            suf_copy(c).wait_recv()
            suf_on(c)

    near_left = jnp.logical_and(has_left, sq < S // 2)
    near_right = jnp.logical_and(has_right, sq >= S // 2)

    def middle(low, high):
        @pl.when(near_left)
        def _():
            pre_pass(low, high)

        @pl.when(near_right)
        def _():
            suf_pass(low, high)

    def middle_far():
        @pl.when(near_left)
        def _():
            suf_pass(0, len(cuts))

        @pl.when(near_right)
        def _():
            pre_pass(0, len(cuts))

    loop(0, 6, backward)
    head_part()
    ends()
    loop(6, KV_HEADS, backward)
    middle(0, len(cuts))
    middle_far()

    @functools.partial(loop, 0, KV_HEADS)
    def _(j):
        g = order(j)

        @pl.when(has_right)
        def _():
            dk_copy(g).wait_recv()
            dv_copy(g).wait_recv()

        w = lanes(g, HD)
        dk_ref[:, w] = (dka[:, w] + dkr[g].astype(F32)).astype(BF16)
        dv_ref[:, w] = (dva[:, w] + dvr[g].astype(F32)).astype(BF16)

    @pl.when(sq == S - 1)
    def _():
        for c in range(len(cuts)):
            pre_copy(c).wait_recv()

    @pl.when(sq == 0)
    def _():
        for c in range(len(cuts)):
            suf_copy(c).wait_recv()

    total = part[...] + pre_in[...].astype(F32) + suf_in[...].astype(F32)
    gh_ref[...] = total[:ACTS].T
    gv_ref[...] = total[ACTS : ACTS + 1]

    @pl.when(has_right)
    def _():
        @functools.partial(loop, 0, KV_HEADS)
        def _(g):
            k_copy(g).wait_send()
            v_copy(g).wait_send()

        for c in range(len(cuts)):
            pre_copy(c).wait_send()

    @pl.when(has_left)
    def _():
        @functools.partial(loop, 0, KV_HEADS)
        def _(g):
            dk_copy(g).wait_send()
            dv_copy(g).wait_send()

        vn_copy().wait_send()
        for c in range(len(cuts)):
            suf_copy(c).wait_send()

    hw_own(0).wait_send()

    @functools.partial(loop, 1, D // 2)
    def _(m):
        hw_copy((dp + D - 2 * m) % D).wait_send()
        hw_pass((dp + 2 * m) % D).wait_send()

    @functools.partial(loop, 1, D)
    def _(m):
        p = (dp + m) % D
        vw_copy(p).wait_send()
        at_copy(p).wait_send()
        st_copy(p).wait_send()


def per_device(D, S, queries, keys, values, head_weight, value_weight, action_ids, rewards, episode_ids):
    FL = head_weight.shape[0]
    qw, kw = HEADS * HD, KV_HEADS * HD
    rows = ACTS + 16
    dma = lambda n: pltpu.SemaphoreType.DMA((n,))
    vm = pltpu.VMEM
    halo = vm((KV_HEADS, BLOCK, HD), BF16)
    vmem = pl.BlockSpec(memory_space=pltpu.VMEM)
    values_row = jnp.broadcast_to(value_weight[None], (16, FL))
    outs = pl.pallas_call(
        functools.partial(kernel, D, S, FL),
        out_shape=(
            jax.ShapeDtypeStruct((BLOCK, qw), BF16),
            jax.ShapeDtypeStruct((BLOCK, kw), BF16),
            jax.ShapeDtypeStruct((BLOCK, kw), BF16),
            jax.ShapeDtypeStruct((FL, ACTS), F32),
            jax.ShapeDtypeStruct((1, FL), F32),
        ),
        in_specs=[pl.BlockSpec(memory_space=pl.ANY)] * 4 + [vmem] * 3 + [pl.BlockSpec(memory_space=pltpu.SMEM)],
        out_specs=(vmem,) * 5,
        scratch_shapes=[
            vm((BLOCK, qw), BF16), vm((BLOCK, kw), BF16), vm((BLOCK, kw), BF16), dma(4),
            halo, halo,
            vm((qw, ACTS), BF16), vm((D * 16, FL), BF16),
            vm((2 * BLOCK, BLOCK), F32), vm((KV_HEADS, 2 * BLOCK, GW), BF16),
            vm((BLOCK, qw), BF16), vm((D * BLOCK, FL), BF16),
            vm((BLOCK, ACTS), F32), vm((BLOCK, BLOCK), F32),
            vm((8, BLOCK), F32), vm((8, BLOCK), F32),
            vm((BLOCK, ACTS), BF16), vm((BLOCK, BLOCK), F32), vm((D * 8, BLOCK), F32),
            vm((rows, D * BLOCK), BF16),
            halo, halo, halo, halo,
            vm((BLOCK, kw), F32), vm((BLOCK, kw), F32),
            vm((rows, FL), F32),
            vm((rows, FL), BF16), vm((rows, FL), BF16), vm((rows, FL), BF16), vm((rows, FL), BF16),
            dma(KV_HEADS), dma(KV_HEADS), dma(KV_HEADS), dma(KV_HEADS),
            dma(D), dma(D), dma(D), dma(D), dma(D), dma(D), dma(D), dma(D), dma(D),
            dma(1), dma(1),
            dma(KV_HEADS), dma(KV_HEADS), dma(KV_HEADS), dma(KV_HEADS),
            dma(4), dma(4), dma(4), dma(4),
        ],
        compiler_params=pltpu.CompilerParams(
            collective_id=0, has_side_effects=True, vmem_limit_bytes=60 * 2**20
        ),
    )(queries[0], keys[0], values[0], head_weight, values_row, action_ids, rewards, episode_ids)
    dq, dk, dv, gh, gv = outs
    return (dq[None], dk[None], dv[None], gh, gv.reshape(FL))


def solution(mesh):
    return jax.shard_map(
        functools.partial(per_device, mesh.shape["dp"], mesh.shape["seq"]),
        mesh=mesh,
        in_specs=(
            P("dp", "seq", None),
            P("dp", "seq", None),
            P("dp", "seq", None),
            P("dp", None),
            P("dp"),
            P("dp", "seq"),
            P("dp", "seq"),
            P("dp", None),
        ),
        out_specs=(
            P("dp", "seq", None),
            P("dp", "seq", None),
            P("dp", "seq", None),
            P("dp", None),
            P("dp"),
        ),
        check_vma=False,
    )
```
